128 devices in a mesh: ctx: 16 (over x, y), db: 8 (over z, core).
Axes of the slice: x: 4, y: 4, z: 4, core: 2. Of those that a mesh axis runs over, the one named last changes fastest.
Arguments:
- states: bfloat16 [4096, 4096], P('ctx', 'db'), may hold values from -60 to 60
- cotangent: bfloat16 [4096, 4096], P('ctx', 'db'), may hold values from -6 to 6
- w_query: bfloat16 [4096, 4096], P(None, 'db'), may hold values from -0.09375 to 0.09375
- w_key: bfloat16 [896, 4096], P(None, 'db'), may hold values from -0.1875 to 0.1875
- w_value: bfloat16 [896, 4096], P(None, 'db'), may hold values from -0.1875 to 0.1875
- w_out: bfloat16 [4096, 4096], P('db'), may hold values from -0.09375 to 0.09375
- database: bfloat16 [768, 128, 896], P('db'), may hold values from -6 to 6
- neighbour_shard: int32 [64, 2], P('ctx'), may hold values from 0 to 7, all different within a row; in each aligned block of 4 rows (0 to 3, 4 to 7, ...) at most 2 rows name the same one
- neighbour_row: int32 [64, 2], P('ctx'), may hold values from 0 to 95
Outputs:
- grad_states: float32 [4096, 4096], P('ctx', 'db')
- grad_database: float32 [768, 128, 896], P('db', 'ctx')
The draws below stay inside these ranges and needn't reach their ends.
Inputs may be any that keep to these rules, and one draw needn't show every extreme that they name: `neighbour_shard`: the 2 neighbours of a span lie in different shards. Among the 4 spans of one index of ctx, at most 2 neighbours lie in one shard, and some shard holds exactly 2.
All inputs are finite; a program needn't handle non-finite values.
Results may differ from the reference program's by a relative error of at most 0.022.
The reference program's roundings to bfloat16 on the way (of `att_states`, `memory`, `query`, `keys`, `grad_out`, `attention_b`, `dscores` and `grad_query`) count: a program that leaves them out, or rounds other values in their place, can miss the bound.
Values may be sent and summed in bfloat16 or wider, within the bound.
No kernel may reach another device: no remote copies, remote signals or barrier semaphores. Data moves between devices by JAX's collectives and lax.ppermute only.
A program may use at most 192 MiB of HBM per device.

```python
import math
import jax
import jax.numpy as jnp
import numpy as np

D = 4096
H = 32
HDIM = 128
DE = 896
CH = 64
R = 128
K = 2
TOK_CTX = 256
DB_SHARD = 96
HD = 4096
TOKENS = 4096
SPANS = 64
DBROWS = 768
CAP = 2
N_DB = 8


def draw_states(key, part):
    key = jax.random.fold_in(key, 11)
    first = jax.random.fold_in(key, 0)
    base = jax.random.truncated_normal(first, -6.0, 6.0, (TOKENS, D), jnp.float32)
    return base.astype(jnp.bfloat16)


def plant(drawn, own_key, low, high):
    spot = [jax.random.randint(jax.random.fold_in(own_key, axis), (), 0, length) for axis, length in enumerate(drawn.shape)]
    widest = drawn.shape.index(max(drawn.shape))
    beside = spot[:widest] + [(spot[widest] + 1) % drawn.shape[widest]] + spot[widest + 1:]
    return drawn.at[tuple(spot)].set(low).at[tuple(beside)].set(high)


def block_scale(rng, dims, cuts, low, high):
    factor_of, own = 1.0, jax.random.fold_in(rng, 6)
    for position, blocks in cuts:
        heights = jnp.exp(jax.random.uniform(jax.random.fold_in(own, position), (blocks,), jnp.float32, low / len(cuts), high / len(cuts)))
        factor_of = factor_of * jnp.repeat(heights, dims[position] // blocks).reshape([-1 if axis == position else 1 for axis in range(len(dims))])
    return factor_of


def deal_out(key, own, number, rows, number_of, top, most, lean):
    order = jax.random.permutation(key, number_of)
    heavy_load, ordinary = portions_of(number_of, rows * top, most, lean, True), portions_of(number_of, rows * top, most, lean, False)
    places = jnp.arange(number_of)

    def named(sizes, turn):
        used = int((sizes > 0).sum())
        fixed = max(1, used // 4)
        moved = fixed + (places - fixed + turn * (used - fixed)) % max(1, number_of - fixed)
        return jnp.zeros((number_of,), jnp.int32).at[order[jnp.where(places < fixed, places, moved)]].set(jnp.asarray(sizes, jnp.int32))

    sizes = jnp.where(number % 4 == 0, named(heavy_load, number // 4), named(ordinary, number - number // 4 - 1))
    mixed = jax.random.permutation(jax.random.fold_in(own, 3), number_of)
    donor, receiver = mixed[0:number_of // 2 * 2:2], mixed[1:number_of // 2 * 2:2]
    slack = jnp.minimum(sizes[donor] - 1, most - sizes[receiver]) // 2
    slack = jnp.where((donor == order[0]) | (receiver == order[0]) | (sizes[receiver] == 0), 0, jnp.maximum(slack, 0))
    moved = jax.random.randint(jax.random.fold_in(own, 4), (number_of // 2,), 0, 1 << 20) % (slack + 1)
    sizes = sizes.at[donor].add(-moved).at[receiver].add(moved)
    members = jnp.searchsorted(jnp.cumsum(sizes), jnp.arange(rows * top), side="right").astype(jnp.int32)
    grid = members.reshape(top, rows).T
    grid = grid[jax.random.permutation(jax.random.fold_in(own, 1), rows)]
    turn = jax.random.randint(jax.random.fold_in(own, 2), (rows, 1), 0, top)
    return jnp.take_along_axis(grid, (jnp.arange(top)[None, :] + turn) % top, axis=1)


def portions_of(count, total, limit, lean, full):
    portions = [(1 << 20) // math.isqrt(grade ** lean) + 1 for grade in range(1, count + 1)]
    largest = limit if full else min(limit, max(-(-total // count), total * portions[0] // sum(portions)))
    least = 1 if total - largest >= count - 1 else 0
    holding, spare = [largest] + [least] * (count - 1), total - largest - least * (count - 1)
    while spare > 0:
        free = [i for i in range(1, count) if holding[i] < largest] or [i for i in range(1, count) if holding[i] < limit]
        mass, left = sum([portions[i] for i in free]), spare
        for i in free:
            more = min(limit - holding[i], max(1, left * portions[i] // mass), spare)
            holding[i] = holding[i] + more
            spare = spare - more
    return np.array(holding)


def centred(stream_key, dims, scale, most, shards=(), dtype=jnp.bfloat16):
    level = block_scale(stream_key, dims, shards, -0.22, 0.18) if shards else 1.0
    result = jax.random.normal(stream_key, dims, jnp.float32) * scale * level
    return jnp.minimum(jnp.maximum(result, -most), most).astype(dtype)


def setup_inputs(seed: int = 0) -> dict:
    arg_keys = jax.random.split(jax.random.key(seed), 10)
    states = draw_states(jax.random.fold_in(arg_keys[9], 71), 0)
    cotangent = centred(arg_keys[1], (TOKENS, D), 1.0, 6.0, ((0, 16), (1, 8)))
    w_query = centred(arg_keys[2], (D, HD), D ** -0.5, 0.09375, ((1, 8),))
    w_key = centred(arg_keys[3], (DE, HD), DE ** -0.5, 0.1875, ((1, 8),))
    w_value = centred(arg_keys[4], (DE, HD), DE ** -0.5, 0.1875, ((1, 8),))
    w_out = centred(arg_keys[5], (HD, D), HD ** -0.5, 0.09375, ((0, 8),))
    database = centred(arg_keys[6], (DBROWS, R, DE), 1.0, 6.0, ((0, 8),))
    neighbour_shard_keys = jax.random.split(jax.random.fold_in(arg_keys[7], 1), SPANS // (TOK_CTX // CH))
    neighbour_shard_turns = jax.random.permutation(jax.random.fold_in(arg_keys[7], 3), SPANS // (TOK_CTX // CH))
    neighbour_shard = jax.vmap(lambda own, number: deal_out(jax.random.fold_in(arg_keys[7], 2), own, number, TOK_CTX // CH, N_DB, K, CAP, 2))(neighbour_shard_keys, neighbour_shard_turns).reshape((SPANS, K))
    neighbour_row = plant(jax.random.randint(arg_keys[8], (SPANS, K), 0, DB_SHARD), jax.random.fold_in(arg_keys[8], 1), 0, DB_SHARD - 1).astype(jnp.int32)
    return dict(states=states, cotangent=cotangent, w_query=w_query, w_key=w_key, w_value=w_value, w_out=w_out, database=database, neighbour_shard=neighbour_shard, neighbour_row=neighbour_row)


def reference(states, cotangent, w_query, w_key, w_value, w_out, database, neighbour_shard, neighbour_row):
    total_rows = states.shape[0]
    span_count = total_rows // CH
    border = CH - 1
    zeros_rows = jnp.zeros((border, D), jnp.bfloat16)
    att_states = jnp.concatenate([states[border:], zeros_rows], 0)
    att_cotangent = jnp.concatenate([cotangent[border:], zeros_rows], 0)
    row_ids = (neighbour_shard * DB_SHARD + neighbour_row).reshape(-1).astype(jnp.int32)
    memory = jnp.take(database, row_ids, axis=0)
    query = jnp.dot(att_states, w_query, preferred_element_type=jnp.float32).astype(jnp.bfloat16)
    flat_memory = memory.reshape(span_count * K * R, DE)
    keys = jnp.dot(flat_memory, w_key, preferred_element_type=jnp.float32).astype(jnp.bfloat16)
    values = jnp.dot(flat_memory, w_value, preferred_element_type=jnp.float32).astype(jnp.bfloat16)
    grad_out = jnp.dot(att_cotangent, w_out.T, preferred_element_type=jnp.float32).astype(jnp.bfloat16)
    query_f = query.astype(jnp.float32).reshape(span_count, CH, H, HDIM)
    keys_f = keys.astype(jnp.float32).reshape(span_count, K * R, H, HDIM)
    values_f = values.astype(jnp.float32).reshape(span_count, K * R, H, HDIM)
    grad_f = grad_out.astype(jnp.float32).reshape(span_count, CH, H, HDIM)
    scale = HDIM ** -0.5
    scores = jnp.einsum("cqhd,ckhd->chqk", query_f, keys_f) * scale
    attention = jax.nn.softmax(scores, axis=-1)
    attention_b = attention.astype(jnp.bfloat16).astype(jnp.float32)
    dattention = jnp.einsum("cqhd,ckhd->chqk", grad_f, values_f)
    dscores = attention * (dattention - jnp.sum(attention * dattention, -1, keepdims=True))
    dscores = dscores.astype(jnp.bfloat16).astype(jnp.float32)
    grad_query = (jnp.einsum("chqk,ckhd->cqhd", dscores, keys_f) * scale).astype(jnp.bfloat16)
    grad_keys = (jnp.einsum("chqk,cqhd->ckhd", dscores, query_f) * scale).astype(jnp.bfloat16)
    grad_values = jnp.einsum("chqk,cqhd->ckhd", attention_b, grad_f).astype(jnp.bfloat16)
    cross = jnp.dot(grad_query.reshape(total_rows, H * HDIM), w_query.T, preferred_element_type=jnp.float32)
    moved = jnp.concatenate([jnp.zeros((border, D), jnp.float32), cross[:total_rows - border]], 0)
    grad_states = cotangent.astype(jnp.float32) + moved
    key_part = jnp.dot(grad_keys.reshape(-1, H * HDIM), w_key.T, preferred_element_type=jnp.float32)
    value_part = jnp.dot(grad_values.reshape(-1, H * HDIM), w_value.T, preferred_element_type=jnp.float32)
    neighbour_grads = (key_part + value_part).reshape(span_count * K, R, DE)
    grad_database = jnp.zeros((database.shape[0], R, DE), jnp.float32).at[row_ids].add(neighbour_grads)
    return grad_states, grad_database
```

```python
import functools

import jax
import jax.numpy as jnp
from jax import lax
from jax.experimental import pallas as pl
from jax.experimental.pallas import tpu as pltpu
from jax.sharding import PartitionSpec as P

HDIM = 128
DE = 896
CH = 64
R = 128
K = 2
CAP = 2
BORDER = CH - 1
SCALE = HDIM ** (-0.5)
BF16, F32 = jnp.bfloat16, jnp.float32
NT = (((1,), (1,)), ((), ()))
TN = (((0,), (0,)), ((), ()))
PLACES = (0, 1, 3, 2)
VMEM = pl.BlockSpec(memory_space=pltpu.VMEM)
SMEM = pl.BlockSpec(memory_space=pltpu.SMEM)
ANY = pl.BlockSpec(memory_space=pl.ANY)


def up(x):
    return lax.ppermute(x, "db", [(s, (s + 2) % 8) for s in range(8)])


def down(x):
    return lax.ppermute(x, "db", [(s, (s - 2) % 8) for s in range(8)])


def across(x):
    return lax.ppermute(x, "db", [(s, s ^ 1) for s in range(8)])


def along_ctx(x, by):
    peers = lax.axis_size("ctx")
    return lax.ppermute(x, "ctx", [(i, i + by) for i in range(peers) if 0 <= i + by < peers])


def shape(dims, dtype=BF16):
    return jax.ShapeDtypeStruct(dims, dtype)


def cost(flops, size):
    return pl.CostEstimate(flops=flops, bytes_accessed=size, transcendentals=0)


def source_of(me, core, place):
    return lax.rem(me // 2 + place, 4) * 2 + (lax.rem(me, 2) + core) % 2


def pack_kernel(a_ref, b_ref, out_ref, sems):
    copies = [
        pltpu.make_async_copy(ref, out_ref.at[at], sems.at[at])
        for at, ref in enumerate((a_ref, b_ref))
    ]
    for copy in copies:
        copy.start()
    for copy in copies:
        copy.wait()


def named(shards, shard):
    count, found = jnp.int32(0), [jnp.int32(0)] * CAP
    for c in range(shards.shape[1]):
        for k in range(K):
            mine = shards[k, c] == shard
            for at in range(CAP):
                found[at] = jnp.where(mine & (count == at), c * K + k, found[at])
            count = count + mine.astype(jnp.int32)
    return found, count


def fetch_kernel(shard_ref, row_ref, database_ref, out_ref, sems):
    found, _ = named(shard_ref, lax.axis_index("db"))
    copies = [
        pltpu.make_async_copy(
            database_ref.at[row_ref[lax.rem(request, K), request // K]],
            out_ref.at[slot],
            sems.at[slot],
        )
        for slot, request in enumerate(found)
    ]
    for copy in copies:
        copy.start()
    for copy in copies:
        copy.wait()


def project_kernel(item, *refs):
    blocks, w_ref, out_ref, full = refs[:8], refs[8], refs[9], refs[10]
    me = lax.axis_index("db")
    width = w_ref.shape[1 - item]
    for index, block in enumerate(blocks):
        core, place = index // 4, PLACES[index % 4]
        spot = pl.multiple_of(source_of(me, core, place) * width, width)
        full[:, pl.ds(spot, width)] = block[...] if place == 2 else block[item]
    rows = full.shape[0]
    if item:
        total = lax.dot_general(full[...], w_ref[...], NT, preferred_element_type=F32)
    else:
        total = jnp.dot(full[...], w_ref[...], preferred_element_type=F32)
    out_ref[...] = pltpu.roll(total, rows - BORDER, 0).astype(BF16)


def attend_kernel(*refs):
    shard_ref, q_ref, q_tail, g_ref, g_tail = refs[:5]
    mems = refs[5:15]
    wk_ref, wv_ref = refs[15:17]
    gq_ref, gk_ref, gv_ref = refs[17:20]
    q_s, g_s, mem_s, k_s, v_s, gq_s = refs[20:]
    me = lax.axis_index("db")
    my_z, my_core = me // 2, lax.rem(me, 2)
    rows, width = q_ref.shape
    spans, heads = rows // CH, width // HDIM
    last = rows - CH
    first_row = lax.broadcasted_iota(jnp.int32, (CH, width), 0) == 0
    for src, tail, dst in ((q_ref, q_tail, q_s), (g_ref, g_tail, g_s)):
        dst[:last] = src[:last]
        dst[last:] = jnp.where(first_row, src[last:], tail[...])

    for c in range(spans):
        for k in range(K):
            request = c * K + k
            shard = shard_ref[k, c]
            rank = jnp.int32(0)
            for earlier in range(request):
                same = shard_ref[earlier % K, earlier // K] == shard
                rank = rank + same.astype(jnp.int32)
            rank = jnp.minimum(rank, CAP - 1)
            core = (lax.rem(shard, 2) + my_core) % 2
            place = lax.rem(shard // 2 - my_z + 4, 4)
            spot = pl.ds(request * R, R)
            for which in range(2):
                own, nxt, prv, far0, far1 = mems[which * 5 : which * 5 + 5]
                here = core == which
                for at, ref in ((0, own), (1, nxt), (3, prv)):

                    @pl.when(here & (place == at))
                    def _(ref=ref, rank=rank, spot=spot):
                        mem_s[spot, :] = ref[rank]

                for at, ref in ((0, far0), (1, far1)):

                    @pl.when(here & (place == 2) & (rank == at))
                    def _(ref=ref, spot=spot):
                        mem_s[spot, :] = ref[...]

    k_s[...] = jnp.dot(mem_s[...], wk_ref[...], preferred_element_type=F32).astype(BF16)
    v_s[...] = jnp.dot(mem_s[...], wv_ref[...], preferred_element_type=F32).astype(BF16)
    for c in range(spans):
        span, memory = pl.ds(c * CH, CH), pl.ds(c * K * R, K * R)
        at = [pl.ds(h * HDIM, HDIM) for h in range(heads)]
        q, g = [q_s[span, x] for x in at], [g_s[span, x] for x in at]
        k, v = [k_s[memory, x] for x in at], [v_s[memory, x] for x in at]
        some = range(heads)
        scores = [
            lax.dot_general(q[h], k[h], NT, preferred_element_type=F32) * SCALE for h in some
        ]
        dattention = [lax.dot_general(g[h], v[h], NT, preferred_element_type=F32) for h in some]
        raised = [jnp.exp(x - jnp.max(x, -1, keepdims=True)) for x in scores]
        attention = [x / jnp.sum(x, -1, keepdims=True) for x in raised]
        mean = [jnp.sum(attention[h] * dattention[h], -1, keepdims=True) for h in some]
        dscores = [(attention[h] * (dattention[h] - mean[h])).astype(BF16) for h in some]
        for h in some:
            gq_s[span, at[h]] = jnp.dot(dscores[h], k[h], preferred_element_type=F32) * SCALE
        for h in some:
            gk = lax.dot_general(dscores[h], q[h], TN, preferred_element_type=F32) * SCALE
            gk_ref[memory, at[h]] = gk.astype(BF16)
        for h in some:
            gv = lax.dot_general(
                attention[h].astype(BF16), g[h], TN, preferred_element_type=F32
            )
            gv_ref[memory, at[h]] = gv.astype(BF16)
    gq_ref[...] = pltpu.roll(gq_s[...], BORDER, 0).astype(BF16)


def term_kernel(core, shard_ref, gk_ref, gv_ref, wk_ref, wv_ref, out_ref):
    me = lax.axis_index("db")
    for place in range(4):
        found, count = named(shard_ref, source_of(me, core, place))
        for slot, request in enumerate(found):

            @pl.when(count > slot)
            def _(place=place, slot=slot, request=request):
                spot = pl.ds(pl.multiple_of(request * R, R), R)
                term = lax.dot_general(gk_ref[spot], wk_ref[...], NT, preferred_element_type=F32)
                term = term + lax.dot_general(
                    gv_ref[spot], wv_ref[...], NT, preferred_element_type=F32
                )
                out_ref[place, slot] = term.astype(BF16)


def cross_kernel(gq_ref, head_ref, w_ref, away_ref, own_ref, full):
    me = lax.axis_index("db")
    rows, width = gq_ref.shape
    last_row = lax.broadcasted_iota(jnp.int32, (CH, width), 0) == CH - 1
    full[:CH] = jnp.where(last_row, gq_ref[:CH], head_ref[...])
    full[CH:] = gq_ref[CH:]
    for core, out in ((1, away_ref), (0, own_ref)):
        for place in range(4):
            spot = pl.multiple_of(source_of(me, core, place) * width, width)
            out[place] = lax.dot_general(
                full[...], w_ref[pl.ds(spot, width), :], NT, preferred_element_type=F32
            ).astype(BF16)


def scatter_kernel(requests, ids_ref, parts_ref, out_ref):
    me = lax.axis_index("db")
    out_ref[...] = jnp.zeros_like(out_ref)

    def group(i, carry):
        count = jnp.int32(0)
        for r in range(requests):
            mine = ids_ref[i, 0, r] == me
            row = ids_ref[i, 0, requests + r]
            slot = jnp.minimum(count, CAP - 1)

            @pl.when(mine)
            def _(row=row, slot=slot):
                out_ref[row] += parts_ref[i * CAP + slot].astype(F32)

            count = count + mine.astype(jnp.int32)
        return carry

    lax.fori_loop(0, ids_ref.shape[0], group, 0)


def gather_blocks(own, early=None):
    nxt, prv = down(own), up(own)
    if early is not None:
        nxt, prv, _ = lax.optimization_barrier((nxt, prv, early))
    far_a, far_b = up(prv[0]), down(nxt[1])
    here = (own, nxt, prv, far_a, far_b)
    return here + tuple(across(x) for x in here)


def add(a, b):
    return (a.astype(F32) + b.astype(F32)).astype(BF16)


def reduce_blocks(own, away, halves):
    got = across(away)
    far_a, far_b = (add(x, y) for x, y in zip(halves(own[2]), halves(got[2])))
    via_up, via_down = up(far_a), down(far_b)
    nxt_a, nxt_b = (add(x, y) for x, y in zip(halves(own[1]), halves(got[1])))
    prv_a, prv_b = (add(x, y) for x, y in zip(halves(own[3]), halves(got[3])))
    nxt = jnp.concatenate([add(nxt_a, via_up), nxt_b], 0)
    prv = jnp.concatenate([prv_a, add(prv_b, via_down)], 0)
    from_prv, from_nxt = up(nxt), down(prv)
    return (own[0].astype(F32) + got[0].astype(F32)) + (
        from_prv.astype(F32) + from_nxt.astype(F32)
    )


def per_device(
    states, cotangent, w_query, w_key, w_value, w_out, database, neighbour_shard, neighbour_row
):
    rows, width = states.shape
    spans = rows // CH
    limit = pltpu.CompilerParams(vmem_limit_bytes=20 * 2**20)
    shards, named_rows = neighbour_shard.T, neighbour_row.T
    peers = lax.axis_size("ctx")

    pair = pl.pallas_call(
        pack_kernel,
        name="pack",
        out_shape=shape((2, rows, width)),
        in_specs=[ANY, ANY],
        out_specs=VMEM,
        scratch_shapes=[pltpu.SemaphoreType.DMA((2,))],
    )(states, cotangent)
    tokens = gather_blocks(pair)
    fetched = pl.pallas_call(
        fetch_kernel,
        name="fetch",
        out_shape=shape((CAP, R, DE)),
        in_specs=[SMEM, SMEM, ANY],
        out_specs=VMEM,
        scratch_shapes=[pltpu.SemaphoreType.DMA((CAP,))],
    )(shards, named_rows, database)
    ids = jnp.concatenate([neighbour_shard.reshape(1, -1), neighbour_row.reshape(1, -1)], 1)
    ids = jnp.pad(ids, ((0, 0), (0, 128 - ids.shape[1])))
    ids = lax.all_to_all(jnp.broadcast_to(ids, (peers, 1, 128)), "ctx", 0, 0, tiled=True)
    memory = gather_blocks(fetched, ids)

    def project(item, w, name):
        blocks = tokens[:3] + tokens[3 + item : 4 + item]
        blocks = blocks + tokens[5:8] + tokens[8 + item : 9 + item]
        return pl.pallas_call(
            functools.partial(project_kernel, item),
            name=name,
            out_shape=shape((rows, width)),
            in_specs=[VMEM] * 9,
            out_specs=VMEM,
            scratch_shapes=[pltpu.VMEM((rows, 8 * width), BF16)],
            compiler_params=limit,
            cost_estimate=cost(2 * rows * width * 8 * width, 16 * rows * width + 16 * width * width),
        )(*blocks, w)

    query = project(0, w_query, "query")
    query_tail = along_ctx(query[rows - CH :], -1)
    grad_out = project(1, w_out, "grad_out")
    grad_tail = along_ctx(grad_out[rows - CH :], -1)
    requests = spans * K
    grad_query, grad_keys, grad_values = pl.pallas_call(
        attend_kernel,
        name="attend",
        out_shape=(shape((rows, width)),) + (shape((requests * R, width)),) * 2,
        in_specs=[SMEM] + [VMEM] * 16,
        out_specs=(VMEM,) * 3,
        scratch_shapes=[
            pltpu.VMEM((rows, width), BF16),
            pltpu.VMEM((rows, width), BF16),
            pltpu.VMEM((requests * R, DE), BF16),
            pltpu.VMEM((requests * R, width), BF16),
            pltpu.VMEM((requests * R, width), BF16),
            pltpu.VMEM((rows, width), F32),
        ],
        compiler_params=limit,
        cost_estimate=cost(8 * requests * R * DE * width, 2**23),
    )(shards, query, query_tail, grad_out, grad_tail, *memory, w_key, w_value)
    head = along_ctx(grad_query[:CH], 1)

    def term(core, name):
        return pl.pallas_call(
            functools.partial(term_kernel, core),
            name=name,
            out_shape=shape((4, CAP, R, DE)),
            in_specs=[SMEM] + [VMEM] * 4,
            out_specs=VMEM,
            compiler_params=limit,
            cost_estimate=cost(2 * requests * R * DE * width, 2**22),
        )(shards, grad_keys, grad_values, w_key, w_value)

    away, own = term(1, "term_away"), term(0, "term_own")
    slots = reduce_blocks(own, away, lambda x: (x[:1], x[1:])).astype(BF16)
    cross_away, cross_own = pl.pallas_call(
        cross_kernel,
        name="cross",
        out_shape=(shape((4, rows, width)), shape((4, rows, width))),
        in_specs=[VMEM] * 3,
        out_specs=(VMEM, VMEM),
        scratch_shapes=[pltpu.VMEM((rows, width), BF16)],
        compiler_params=limit,
        cost_estimate=cost(2 * rows * width * 8 * width, 2**23),
    )(grad_query, head, w_query)
    half = rows // 2
    cross = reduce_blocks(cross_own, cross_away, lambda x: (x[:half], x[half:]))
    grad_states = cotangent.astype(F32) + cross

    block = R // peers
    spread = slots.reshape(CAP, peers, block, DE).transpose(1, 0, 2, 3)
    parts = lax.all_to_all(spread, "ctx", 0, 0, tiled=True).reshape(peers * CAP, block, DE)
    grad_database = pl.pallas_call(
        functools.partial(scatter_kernel, requests),
        name="scatter",
        out_shape=shape((database.shape[0], block, DE), F32),
        in_specs=[SMEM, VMEM],
        out_specs=VMEM,
        compiler_params=limit,
    )(ids, parts)
    return grad_states, grad_database


def solution(mesh):
    in_specs = (
        P("ctx", "db"),
        P("ctx", "db"),
        P(None, "db"),
        P(None, "db"),
        P(None, "db"),
        P("db", None),
        P("db", None, None),
        P("ctx", None),
        P("ctx", None),
    )
    out_specs = (P("ctx", "db"), P("db", "ctx", None))
    return jax.shard_map(
        per_device, mesh=mesh, in_specs=in_specs, out_specs=out_specs, check_vma=False
    )
```

```python
import functools

import jax
import jax.numpy as jnp
from jax import lax
from jax.experimental import pallas as pl
from jax.experimental.pallas import tpu as pltpu
from jax.sharding import PartitionSpec as P

HDIM = 128
DE = 896
CH = 64
R = 128
K = 2
CAP = 2
BORDER = CH - 1
SCALE = HDIM ** (-0.5)
BF16, F32 = jnp.bfloat16, jnp.float32
NT = (((1,), (1,)), ((), ()))
TN = (((0,), (0,)), ((), ()))
VMEM = pl.BlockSpec(memory_space=pltpu.VMEM)
SMEM = pl.BlockSpec(memory_space=pltpu.SMEM)
ANY = pl.BlockSpec(memory_space=pl.ANY)
HBM = pl.BlockSpec(memory_space=pltpu.HBM)


def up(x):
    return lax.ppermute(x, "db", [(s, (s + 2) % 8) for s in range(8)])


def down(x):
    return lax.ppermute(x, "db", [(s, (s - 2) % 8) for s in range(8)])


def across(x):
    return lax.ppermute(x, "db", [(s, s ^ 1) for s in range(8)])


def along_ctx(x, by):
    peers = lax.axis_size("ctx")
    return lax.ppermute(x, "ctx", [(i, i + by) for i in range(peers) if 0 <= i + by < peers])


def shape(dims, dtype=BF16):
    return jax.ShapeDtypeStruct(dims, dtype)


def cost(flops, size):
    return pl.CostEstimate(flops=flops, bytes_accessed=size, transcendentals=0)


def source_of(me, core, place):
    return lax.rem(me // 2 + place, 4) * 2 + (lax.rem(me, 2) + core) % 2


def named(shards, shard):
    count, found = jnp.int32(0), [jnp.int32(0)] * CAP
    for c in range(shards.shape[1]):
        for k in range(K):
            mine = shards[k, c] == shard
            for at in range(CAP):
                found[at] = jnp.where(mine & (count == at), c * K + k, found[at])
            count = count + mine.astype(jnp.int32)
    return found, count


def load_kernel(
    shard_ref, row_ref, states_ref, cotangent_ref, database_ref, out_ref, label_ref, sems
):
    rows, width = states_ref.shape
    copies = []

    def copy(source, at, item, start, size):
        count = source.shape[-1] // HDIM
        for j in range(count):
            copies.append(
                pltpu.make_async_copy(
                    source.at[:, pl.ds(j * HDIM, HDIM)],
                    out_ref.at[item, pl.ds(start + j * size, size)],
                    sems.at[at + j],
                )
            )
            copies[-1].start()

    copy(states_ref, 0, 0, 0, rows)
    copy(cotangent_ref, 4, 1, 0, rows)
    found, count = named(shard_ref, lax.axis_index("db"))
    named_rows = [row_ref[lax.rem(request, K), request // K] for request in found]
    for slot, row in enumerate(named_rows):
        copy(database_ref.at[row], 8 + 7 * slot, slot, rows * width // HDIM, R)
    for slot, row in enumerate(named_rows):
        label = jnp.where(count > slot, row, -1).astype(F32)
        label_ref[slot] = jnp.full(label_ref.shape[1:], label, F32)
    for each in copies:
        each.wait()


def hold_kernel(label_ref, a_ref, b_ref, a_out, b_out, done_ref, sems):
    copies = [
        pltpu.make_async_copy(src, dst, sems.at[at])
        for at, (src, dst) in enumerate(((a_ref, a_out), (b_ref, b_out)))
    ]
    for copy in copies:
        copy.start()
    for copy in copies:
        copy.wait()
    done_ref[...] = label_ref[...]


def project_kernel(*refs):
    blocks, weights, outs, tail_ref, full = refs[:10], refs[10:12], refs[12:14], *refs[14:]
    me = lax.axis_index("db")
    rows, width = outs[0].shape
    for item in range(2):
        for core in range(2):
            own, nxt, prv, *far = blocks[core * 5 : core * 5 + 5]
            for place, block in ((0, own), (1, nxt), (3, prv), (2, far[item])):
                spot = pl.multiple_of(source_of(me, core, place) * width, width)
                for j in range(width // HDIM):
                    part = pl.ds(j * rows, rows)
                    full[item, :, pl.ds(spot + j * HDIM, HDIM)] = (
                        block[part] if place == 2 else block[item, part]
                    )
    for item in range(2):
        w = weights[item][...]
        if item:
            total = lax.dot_general(full[item], w, NT, preferred_element_type=F32)
        else:
            total = jnp.dot(full[item], w, preferred_element_type=F32)
        total = pltpu.roll(total, rows - BORDER, 0).astype(BF16)
        outs[item][...] = total
        tail_ref[item] = total[rows - CH :]


def places_of(shard_ref):
    me = lax.axis_index("db")
    found = []
    for request in range(shard_ref.shape[1] * K):
        shard = shard_ref[request % K, request // K]
        rank = jnp.int32(0)
        for earlier in range(request):
            same = shard_ref[earlier % K, earlier // K] == shard
            rank = rank + same.astype(jnp.int32)
        core = (lax.rem(shard, 2) + lax.rem(me, 2)) % 2
        place = lax.rem(shard // 2 - me // 2 + 4, 4)
        found.append((core, place, jnp.minimum(rank, CAP - 1)))
    return found


def span_gradients(q, g, k_ref, v_ref, memory, gk_ref, gv_ref):
    some = range(len(q))
    at = [pl.ds(h * HDIM, HDIM) for h in some]
    k, v = [k_ref[memory, x] for x in at], [v_ref[memory, x] for x in at]
    scores = [lax.dot_general(q[h], k[h], NT, preferred_element_type=F32) * SCALE for h in some]
    dattention = [lax.dot_general(g[h], v[h], NT, preferred_element_type=F32) for h in some]
    raised = [jnp.exp(x - jnp.max(x, -1, keepdims=True)) for x in scores]
    attention = [x / jnp.sum(x, -1, keepdims=True) for x in raised]
    mean = [jnp.sum(attention[h] * dattention[h], -1, keepdims=True) for h in some]
    dscores = [(attention[h] * (dattention[h] - mean[h])).astype(BF16) for h in some]
    gq = [jnp.dot(dscores[h], k[h], preferred_element_type=F32) * SCALE for h in some]
    for h in some:
        gk = lax.dot_general(dscores[h], q[h], TN, preferred_element_type=F32) * SCALE
        gk_ref[memory, at[h]] = gk.astype(BF16)
    for h in some:
        gv = lax.dot_general(attention[h].astype(BF16), g[h], TN, preferred_element_type=F32)
        gv_ref[memory, at[h]] = gv.astype(BF16)
    return gq


def neighbour_terms(gk_ref, gv_ref, wk_ref, wv_ref, found, term_s, away_ref, own_ref):
    term = lax.dot_general(gk_ref[...], wk_ref[...], NT, preferred_element_type=F32)
    term = term + lax.dot_general(gv_ref[...], wv_ref[...], NT, preferred_element_type=F32)
    term_s[...] = term.astype(BF16)
    for at, (core, place, rank) in enumerate(found):
        spot = pl.ds(at * R, R)
        for which, ref in ((0, own_ref), (1, away_ref)):

            @pl.when(core == which)
            def _(spot=spot, place=place, rank=rank, ref=ref):
                ref[place, rank] = term_s[spot]


def attend_kernel(*refs):
    shard_ref, mems, wk_ref, wv_ref, q_ref, g_ref = refs[0], refs[1:11], *refs[11:15]
    k_ref, v_ref, gq_ref, away_ref, own_ref = refs[15:20]
    mem_s, k_s, v_s, gk_s, gv_s, term_s = refs[20:]
    rows, width = q_ref.shape
    spans = rows // CH
    found = places_of(shard_ref)
    base = rows * width // HDIM

    def take(request, read):
        for j in range(DE // HDIM):
            part = read(pl.ds(base + j * R, R))
            mem_s[pl.ds(request * R, R), pl.ds(j * HDIM, HDIM)] = part

    for request, (core, place, rank) in enumerate(found):
        for which in range(2):
            own, nxt, prv, far0, far1 = mems[which * 5 : which * 5 + 5]
            here = core == which
            for at, ref in ((0, own), (1, nxt), (3, prv)):

                @pl.when(here & (place == at))
                def _(ref=ref, rank=rank, request=request):
                    take(request, lambda part: ref[rank, part])

            for at, ref in ((0, far0), (1, far1)):

                @pl.when(here & (place == 2) & (rank == at))
                def _(ref=ref, request=request):
                    take(request, lambda part: ref[part])

    k_s[...] = jnp.dot(mem_s[...], wk_ref[...], preferred_element_type=F32).astype(BF16)
    v_s[...] = jnp.dot(mem_s[...], wv_ref[...], preferred_element_type=F32).astype(BF16)
    heads = [pl.ds(h * HDIM, HDIM) for h in range(width // HDIM)]
    for c in range(spans - 1):
        span, memory = pl.ds(c * CH, CH), pl.ds(c * K * R, K * R)
        q, g = [q_ref[span, x] for x in heads], [g_ref[span, x] for x in heads]
        gq = span_gradients(q, g, k_s, v_s, memory, gk_s, gv_s)
        for x, value in zip(heads, gq):
            gq_ref[span, x] = value
    memory = pl.ds((spans - 1) * K * R, K * R)
    k_ref[...], v_ref[...] = k_s[memory], v_s[memory]
    first = found[: (spans - 1) * K]
    neighbour_terms(gk_s, gv_s, wk_ref, wv_ref, first, term_s, away_ref, own_ref)


def last_kernel(*refs):
    shard_ref, q_ref, g_ref, tail_ref, k_ref, v_ref, wk_ref, wv_ref, gq_in = refs[:9]
    gq_ref, away_ref, own_ref = refs[11:14]
    gk_s, gv_s, term_s = refs[14:]
    rows, width = q_ref.shape
    last = rows - CH
    heads = [pl.ds(h * HDIM, HDIM) for h in range(width // HDIM)]
    first_row = lax.broadcasted_iota(jnp.int32, (CH, HDIM), 0) == 0
    q, g = (
        [jnp.where(first_row, ref[last:, x], tail_ref[item, :, x]) for x in heads]
        for item, ref in enumerate((q_ref, g_ref))
    )
    gq = span_gradients(q, g, k_ref, v_ref, pl.ds(0, K * R), gk_s, gv_s)
    gq_ref[:last] = gq_in[...].astype(BF16)
    for x, value in zip(heads, gq):
        gq_ref[last:, x] = value.astype(BF16)
    found = places_of(shard_ref)[-K:]
    neighbour_terms(gk_s, gv_s, wk_ref, wv_ref, found, term_s, away_ref, own_ref)


def cross_kernel(gq_ref, w_ref, away_ref, own_ref):
    me = lax.axis_index("db")
    width = gq_ref.shape[1]
    for core, out in ((1, away_ref), (0, own_ref)):
        for place in range(4):
            spot = pl.multiple_of(source_of(me, core, place) * width, width)
            out[place] = lax.dot_general(
                gq_ref[...], w_ref[pl.ds(spot, width), :], NT, preferred_element_type=F32
            ).astype(BF16)


def scatter_kernel(label_ref, parts_ref, out_ref):
    out_ref[...] = jnp.zeros_like(out_ref)
    width = out_ref.shape[2]

    def item(i, carry):
        row = label_ref[i]

        @pl.when(row >= 0)
        def _():
            out_ref[row] += parts_ref[i][:, :width].astype(F32)

        return carry

    lax.fori_loop(0, parts_ref.shape[0], item, 0)


def after(x, token):
    return x + jnp.where(token > 0, -0.0, 0.0).astype(x.dtype)


def gather_two(own, token):
    nxt, prv = down(own), up(own)
    return own, nxt, prv, up(after(prv[0], token)), down(after(nxt[1], token))


def with_other_core(blocks):
    return tuple(blocks) + tuple(across(x) for x in blocks)


def add(*parts):
    return functools.reduce(lambda a, b: a + b, [x.astype(F32) for x in parts])


def far_sums(own, got, half):
    return add(own[2][:half], got[2][:half]), add(own[2][half:], got[2][half:])


def near_sums(own, got, half, far_up, far_down):
    nxt = [add(own[1][:half], got[1][:half], far_up), add(own[1][half:], got[1][half:])]
    prv = [add(own[3][:half], got[3][:half]), add(own[3][half:], got[3][half:], far_down)]
    return jnp.concatenate(nxt, 0), jnp.concatenate(prv, 0)


def per_device(
    states, cotangent, w_query, w_key, w_value, w_out, database, neighbour_shard, neighbour_row
):
    rows, width = states.shape
    spans = rows // CH
    limit = pltpu.CompilerParams(vmem_limit_bytes=20 * 2**20)
    shards, named_rows = neighbour_shard.T, neighbour_row.T
    peers = lax.axis_size("ctx")

    given_rows = rows * width // HDIM + R * DE // HDIM
    given, label = pl.pallas_call(
        load_kernel,
        name="load",
        out_shape=(shape((2, given_rows, HDIM)), shape((CAP, 8, 128), F32)),
        in_specs=[SMEM, SMEM, ANY, ANY, ANY],
        out_specs=(VMEM, VMEM),
        scratch_shapes=[pltpu.SemaphoreType.DMA((2 * (width + DE) // HDIM,))],
    )(shards, named_rows, states, cotangent, database)
    *held, done = pl.pallas_call(
        hold_kernel,
        name="hold",
        out_shape=(shape(w_query.shape), shape(w_out.shape), shape(label.shape, F32)),
        in_specs=[VMEM, HBM, HBM],
        out_specs=(VMEM,) * 3,
        scratch_shapes=[pltpu.SemaphoreType.DMA((2,))],
        compiler_params=limit,
    )(label, w_query, w_out)
    gathered = with_other_core(gather_two(given, done[0, :1]))

    query, grad_out, tails = pl.pallas_call(
        project_kernel,
        name="project",
        out_shape=(shape((rows, width)), shape((rows, width)), shape((2, CH, width))),
        in_specs=[VMEM] * 12,
        out_specs=(VMEM,) * 3,
        scratch_shapes=[pltpu.VMEM((2, rows, 8 * width), BF16)],
        compiler_params=limit,
        cost_estimate=cost(32 * rows * width * width, 2**23),
    )(*gathered, *held)
    tails = along_ctx(tails, -1)
    positions, slots_of = spans * K * R, shape((4, CAP, R, DE))
    most = positions - K * R
    *last, away, own = pl.pallas_call(
        attend_kernel,
        name="attend",
        out_shape=(shape((K * R, width)), shape((K * R, width)), shape((rows - CH, width), F32))
        + (slots_of, slots_of),
        in_specs=[SMEM] + [VMEM] * 14,
        out_specs=(VMEM,) * 5,
        scratch_shapes=[
            pltpu.VMEM((positions, DE), BF16),
            pltpu.VMEM((positions, width), BF16),
            pltpu.VMEM((positions, width), BF16),
            pltpu.VMEM((most, width), BF16),
            pltpu.VMEM((most, width), BF16),
            pltpu.VMEM((most, DE), BF16),
        ],
        compiler_params=limit,
        cost_estimate=cost(8 * positions * DE * width, 2**23),
    )(shards, *gathered, w_key, w_value, query, grad_out)
    grad_query, away, own = pl.pallas_call(
        last_kernel,
        name="last",
        out_shape=(shape((rows, width)), slots_of, slots_of),
        in_specs=[SMEM] + [VMEM] * 8 + [VMEM] * 2,
        out_specs=(VMEM,) * 3,
        scratch_shapes=[
            pltpu.VMEM((K * R, width), BF16),
            pltpu.VMEM((K * R, width), BF16),
            pltpu.VMEM((K * R, DE), BF16),
        ],
        input_output_aliases={9: 1, 10: 2},
        compiler_params=limit,
        cost_estimate=cost(2 * positions * DE * width, 2**22),
    )(shards, query, grad_out, tails, last[0], last[1], w_key, w_value, last[2], away, own)
    got, half = across(away), CAP // 2
    far_up, far_down = far_sums(own, got, half)
    far_up, far_down = up(far_up.astype(BF16)), down(far_down.astype(BF16))
    nxt, prv = (x.astype(BF16) for x in near_sums(own, got, half, far_up, far_down))
    slots = add(own[0], got[0], up(nxt), down(prv)).astype(BF16)
    block = R // peers
    spread = slots.reshape(CAP, peers, block, DE).transpose(1, 0, 2, 3)
    labels = jnp.broadcast_to(label.astype(BF16), (peers,) + label.shape)
    spread = jnp.concatenate([spread, labels], -1)
    parts = lax.all_to_all(spread, "ctx", 0, 0, tiled=True)
    parts = parts.reshape(peers * CAP, block, DE + label.shape[-1])
    labels = parts[:, 0, DE].astype(jnp.int32)
    cross_away, cross_own = pl.pallas_call(
        cross_kernel,
        name="cross",
        out_shape=(shape((4, rows, width)), shape((4, rows, width))),
        in_specs=[VMEM] * 2,
        out_specs=(VMEM, VMEM),
        compiler_params=limit,
        cost_estimate=cost(2 * rows * width * 8 * width, 2**23),
    )(grad_query, held[0])
    cross_got, half = across(cross_away), rows // 2
    far_up, far_down = far_sums(cross_own, cross_got, half)
    far_up, far_down = up(far_up.astype(BF16)), down(far_down.astype(BF16))
    nxt, prv = near_sums(cross_own, cross_got, half, far_up, far_down)
    nxt, prv = nxt.astype(BF16), prv.astype(BF16)
    cross = add(cross_own[0], cross_got[0], up(nxt), down(prv))
    keep = rows - BORDER
    carried = along_ctx(cross[keep:].astype(BF16), 1).astype(F32)
    grad_states = cotangent.astype(F32) + jnp.concatenate([carried, cross[:keep]], 0)
    grad_database = pl.pallas_call(
        scatter_kernel,
        name="scatter",
        out_shape=shape((database.shape[0], block, DE), F32),
        in_specs=[SMEM, VMEM],
        out_specs=VMEM,
        compiler_params=limit,
        cost_estimate=cost(2**38, 2**32),
    )(labels, parts)
    return grad_states, grad_database


def solution(mesh):
    in_specs = (
        P("ctx", "db"),
        P("ctx", "db"),
        P(None, "db"),
        P(None, "db"),
        P(None, "db"),
        P("db", None),
        P("db", None, None),
        P("ctx", None),
        P("ctx", None),
    )
    out_specs = (P("ctx", "db"), P("db", "ctx", None))
    return jax.shard_map(
        per_device, mesh=mesh, in_specs=in_specs, out_specs=out_specs, check_vma=False
    )
```

```python
import functools

import jax
import jax.numpy as jnp
from jax import lax
from jax.experimental import pallas as pl
from jax.experimental.pallas import tpu as pltpu
from jax.sharding import PartitionSpec as P

HDIM = 128
DE = 896
CH = 64
R = 128
K = 2
CAP = 2
BORDER = CH - 1
SCALE = HDIM ** (-0.5)
BF16, F32 = jnp.bfloat16, jnp.float32
NT = (((1,), (1,)), ((), ()))
TN = (((0,), (0,)), ((), ()))
VMEM = pl.BlockSpec(memory_space=pltpu.VMEM)
SMEM = pl.BlockSpec(memory_space=pltpu.SMEM)
ANY = pl.BlockSpec(memory_space=pl.ANY)


def up(x):
    return lax.ppermute(x, "db", [(s, (s + 2) % 8) for s in range(8)])


def down(x):
    return lax.ppermute(x, "db", [(s, (s - 2) % 8) for s in range(8)])


def across(x):
    return lax.ppermute(x, "db", [(s, s ^ 1) for s in range(8)])


def along_ctx(x, by):
    peers = lax.axis_size("ctx")
    return lax.ppermute(x, "ctx", [(i, i + by) for i in range(peers) if 0 <= i + by < peers])


def shape(dims, dtype=BF16):
    return jax.ShapeDtypeStruct(dims, dtype)


def cost(flops, size):
    return pl.CostEstimate(flops=flops, bytes_accessed=size, transcendentals=0)


def source_of(me, core, place):
    return lax.rem(me // 2 + place, 4) * 2 + (lax.rem(me, 2) + core) % 2


def named(shards, shard):
    count, found = jnp.int32(0), [jnp.int32(0)] * CAP
    for c in range(shards.shape[1]):
        for k in range(K):
            mine = shards[k, c] == shard
            for at in range(CAP):
                found[at] = jnp.where(mine & (count == at), c * K + k, found[at])
            count = count + mine.astype(jnp.int32)
    return found, count


def load_kernel(
    shard_ref, row_ref, states_ref, cotangent_ref, database_ref, out_ref, label_ref, sems
):
    rows, width = states_ref.shape
    copies = []

    def copy(source, at, item, start, size):
        count = source.shape[-1] // HDIM
        for j in range(count):
            copies.append(
                pltpu.make_async_copy(
                    source.at[:, pl.ds(j * HDIM, HDIM)],
                    out_ref.at[item, pl.ds(start + j * size, size)],
                    sems.at[at + j],
                )
            )
            copies[-1].start()

    copy(states_ref, 0, 0, 0, rows)
    copy(cotangent_ref, 4, 1, 0, rows)
    found, count = named(shard_ref, lax.axis_index("db"))
    named_rows = [row_ref[lax.rem(request, K), request // K] for request in found]
    for slot, row in enumerate(named_rows):
        copy(database_ref.at[row], 8 + 7 * slot, slot, rows * width // HDIM, R)
    for slot, row in enumerate(named_rows):
        label = jnp.where(count > slot, row, -1).astype(F32)
        label_ref[slot] = jnp.full(label_ref.shape[1:], label, F32)
    for each in copies:
        each.wait()


def near_kernel(*refs):
    blocks, weights, (wk_ref, wv_ref) = refs[:6], refs[6:8], refs[8:10]
    (sum_ref, k_ref, v_ref), (full, mem_s) = refs[10:13], refs[13:]
    me = lax.axis_index("db")
    rows, width = sum_ref.shape[1:]
    base = rows * width // HDIM
    for core in range(2):
        far = pl.multiple_of(source_of(me, core, 2) * width, width)
        full[:, :, pl.ds(far, width)] = jnp.zeros((2, rows, width), BF16)
        for at, place in enumerate((0, 1, 3)):
            block = blocks[core * 3 + at]
            spot = pl.multiple_of(source_of(me, core, place) * width, width)
            for item in range(2):
                for j in range(width // HDIM):
                    full[item, :, pl.ds(spot + j * HDIM, HDIM)] = block[item, pl.ds(j * rows, rows)]
                slot = ((core * 3 + at) * 2 + item) * R
                for j in range(DE // HDIM):
                    part = block[item, pl.ds(base + j * R, R)]
                    mem_s[pl.ds(slot, R), pl.ds(j * HDIM, HDIM)] = part
    sum_ref[0] = jnp.dot(full[0], weights[0][...], preferred_element_type=F32)
    sum_ref[1] = lax.dot_general(full[1], weights[1][...], NT, preferred_element_type=F32)
    k_ref[...] = jnp.dot(mem_s[...], wk_ref[...], preferred_element_type=F32).astype(BF16)
    v_ref[...] = jnp.dot(mem_s[...], wv_ref[...], preferred_element_type=F32).astype(BF16)


def project_kernel(*refs):
    fars, weights, sum_ref, outs, tail_ref, x_s = refs[:4], refs[4:6], refs[6], refs[7:9], *refs[9:]
    me = lax.axis_index("db")
    rows, width = outs[0].shape
    for item in range(2):
        total = sum_ref[item]
        for core in range(2):
            for j in range(width // HDIM):
                x_s[:, pl.ds(j * HDIM, HDIM)] = fars[core * 2 + item][pl.ds(j * rows, rows)]
            spot = pl.ds(pl.multiple_of(source_of(me, core, 2) * width, width), width)
            if item:
                part = lax.dot_general(
                    x_s[...], weights[1][:, spot], NT, preferred_element_type=F32
                )
            else:
                part = jnp.dot(x_s[...], weights[0][spot, :], preferred_element_type=F32)
            total = total + part
        total = pltpu.roll(total, rows - BORDER, 0).astype(BF16)
        outs[item][...] = total
        tail_ref[item] = total[rows - CH :]


def places_of(shard_ref):
    me = lax.axis_index("db")
    found = []
    for request in range(shard_ref.shape[1] * K):
        shard = shard_ref[request % K, request // K]
        rank = jnp.int32(0)
        for earlier in range(request):
            same = shard_ref[earlier % K, earlier // K] == shard
            rank = rank + same.astype(jnp.int32)
        core = (lax.rem(shard, 2) + lax.rem(me, 2)) % 2
        place = lax.rem(shard // 2 - me // 2 + 4, 4)
        found.append((core, place, jnp.minimum(rank, CAP - 1)))
    return found


def span_gradients(q, g, k_ref, v_ref, memory, gk_ref, gv_ref):
    some = range(len(q))
    at = [pl.ds(h * HDIM, HDIM) for h in some]
    k, v = [k_ref[memory, x] for x in at], [v_ref[memory, x] for x in at]
    scores = [lax.dot_general(q[h], k[h], NT, preferred_element_type=F32) * SCALE for h in some]
    dattention = [lax.dot_general(g[h], v[h], NT, preferred_element_type=F32) for h in some]
    raised = [jnp.exp(x - jnp.max(x, -1, keepdims=True)) for x in scores]
    attention = [x / jnp.sum(x, -1, keepdims=True) for x in raised]
    mean = [jnp.sum(attention[h] * dattention[h], -1, keepdims=True) for h in some]
    dscores = [(attention[h] * (dattention[h] - mean[h])).astype(BF16) for h in some]
    gq = [jnp.dot(dscores[h], k[h], preferred_element_type=F32) * SCALE for h in some]
    for h in some:
        gk = lax.dot_general(dscores[h], q[h], TN, preferred_element_type=F32) * SCALE
        gk_ref[memory, at[h]] = gk.astype(BF16)
    for h in some:
        gv = lax.dot_general(attention[h].astype(BF16), g[h], TN, preferred_element_type=F32)
        gv_ref[memory, at[h]] = gv.astype(BF16)
    return gq


def neighbour_terms(gk_ref, gv_ref, wk_ref, wv_ref, found, term_s, away_ref, own_ref):
    term = lax.dot_general(gk_ref[...], wk_ref[...], NT, preferred_element_type=F32)
    term = term + lax.dot_general(gv_ref[...], wv_ref[...], NT, preferred_element_type=F32)
    term_s[...] = term.astype(BF16)
    for at, (core, place, rank) in enumerate(found):
        spot = pl.ds(at * R, R)
        for which, ref in ((0, own_ref), (1, away_ref)):

            @pl.when(core == which)
            def _(spot=spot, place=place, rank=rank, ref=ref):
                ref[place, rank] = term_s[spot]


def attend_kernel(*refs):
    shard_ref, fars, k_near, v_near, wk_ref, wv_ref, q_ref, g_ref = refs[0], refs[1:5], *refs[5:11]
    k_ref, v_ref, gq_ref, away_ref, own_ref = refs[11:16]
    mem_s, k_far, v_far, k_s, v_s, gk_s, gv_s, term_s = refs[16:]
    rows, width = q_ref.shape
    spans = rows // CH
    base = rows * width // HDIM
    for slot, far in enumerate(fars):
        for j in range(DE // HDIM):
            part = far[pl.ds(base + j * R, R)]
            mem_s[pl.ds(slot * R, R), pl.ds(j * HDIM, HDIM)] = part
    k_far[...] = jnp.dot(mem_s[...], wk_ref[...], preferred_element_type=F32).astype(BF16)
    v_far[...] = jnp.dot(mem_s[...], wv_ref[...], preferred_element_type=F32).astype(BF16)
    found = places_of(shard_ref)
    for request, (core, place, rank) in enumerate(found):
        spot = pl.ds(request * R, R)

        @pl.when(place == 2)
        def _(spot=spot, slot=core * 2 + rank):
            source = pl.ds(pl.multiple_of(slot * R, R), R)
            k_s[spot], v_s[spot] = k_far[source], v_far[source]

        @pl.when(place != 2)
        def _(spot=spot, slot=(core * 3 + jnp.minimum(place, 2)) * 2 + rank):
            source = pl.ds(pl.multiple_of(slot * R, R), R)
            k_s[spot], v_s[spot] = k_near[source], v_near[source]

    heads = [pl.ds(h * HDIM, HDIM) for h in range(width // HDIM)]
    for c in range(spans - 1):
        span, memory = pl.ds(c * CH, CH), pl.ds(c * K * R, K * R)
        q, g = [q_ref[span, x] for x in heads], [g_ref[span, x] for x in heads]
        gq = span_gradients(q, g, k_s, v_s, memory, gk_s, gv_s)
        for x, value in zip(heads, gq):
            gq_ref[span, x] = value
    memory = pl.ds((spans - 1) * K * R, K * R)
    k_ref[...], v_ref[...] = k_s[memory], v_s[memory]
    first = found[: (spans - 1) * K]
    neighbour_terms(gk_s, gv_s, wk_ref, wv_ref, first, term_s, away_ref, own_ref)


def last_kernel(*refs):
    shard_ref, q_ref, g_ref, tail_ref, k_ref, v_ref, wk_ref, wv_ref, gq_in = refs[:9]
    gq_ref, away_ref, own_ref = refs[11:14]
    gk_s, gv_s, term_s = refs[14:]
    rows, width = q_ref.shape
    last = rows - CH
    heads = [pl.ds(h * HDIM, HDIM) for h in range(width // HDIM)]
    first_row = lax.broadcasted_iota(jnp.int32, (CH, HDIM), 0) == 0
    q, g = (
        [jnp.where(first_row, ref[last:, x], tail_ref[item, :, x]) for x in heads]
        for item, ref in enumerate((q_ref, g_ref))
    )
    gq = span_gradients(q, g, k_ref, v_ref, pl.ds(0, K * R), gk_s, gv_s)
    gq_ref[:last] = gq_in[...].astype(BF16)
    for x, value in zip(heads, gq):
        gq_ref[last:, x] = value.astype(BF16)
    found = places_of(shard_ref)[-K:]
    neighbour_terms(gk_s, gv_s, wk_ref, wv_ref, found, term_s, away_ref, own_ref)


def cross_kernel(gq_ref, w_ref, away_ref, own_ref):
    me = lax.axis_index("db")
    width = gq_ref.shape[1]
    for core, out in ((1, away_ref), (0, own_ref)):
        for place in range(4):
            spot = pl.multiple_of(source_of(me, core, place) * width, width)
            out[place] = lax.dot_general(
                gq_ref[...], w_ref[pl.ds(spot, width), :], NT, preferred_element_type=F32
            ).astype(BF16)


def scatter_kernel(label_ref, parts_ref, out_ref):
    out_ref[...] = jnp.zeros_like(out_ref)
    width = out_ref.shape[2]

    def item(i, carry):
        row = label_ref[i]

        @pl.when(row >= 0)
        def _():
            out_ref[row] += parts_ref[i][:, :width].astype(F32)

        return carry

    lax.fori_loop(0, parts_ref.shape[0], item, 0)


def after(x, token):
    return x + jnp.where(token > 0, -0.0, 0.0).astype(x.dtype)


def add(*parts):
    return functools.reduce(lambda a, b: a + b, [x.astype(F32) for x in parts])


def far_sums(own, got, half):
    return add(own[2][:half], got[2][:half]), add(own[2][half:], got[2][half:])


def near_sums(own, got, half, far_up, far_down):
    nxt = [add(own[1][:half], got[1][:half], far_up), add(own[1][half:], got[1][half:])]
    prv = [add(own[3][:half], got[3][:half]), add(own[3][half:], got[3][half:], far_down)]
    return jnp.concatenate(nxt, 0), jnp.concatenate(prv, 0)


def per_device(
    states, cotangent, w_query, w_key, w_value, w_out, database, neighbour_shard, neighbour_row
):
    rows, width = states.shape
    spans = rows // CH
    limit = pltpu.CompilerParams(vmem_limit_bytes=20 * 2**20)
    shards, named_rows = neighbour_shard.T, neighbour_row.T
    peers = lax.axis_size("ctx")

    given_rows = rows * width // HDIM + R * DE // HDIM
    given, label = pl.pallas_call(
        load_kernel,
        name="load",
        out_shape=(shape((2, given_rows, HDIM)), shape((CAP, 8, 128), F32)),
        in_specs=[SMEM, SMEM, ANY, ANY, ANY],
        out_specs=(VMEM, VMEM),
        scratch_shapes=[pltpu.SemaphoreType.DMA((2 * (width + DE) // HDIM,))],
    )(shards, named_rows, states, cotangent, database)
    nxt, prv = down(given), up(given)
    far_a, far_b = up(prv[0]), down(nxt[1])
    near = (given, nxt, prv, across(given), across(nxt), across(prv))
    partial, *near_states = pl.pallas_call(
        near_kernel,
        name="near",
        out_shape=(shape((2, rows, width), F32),) + (shape((12 * R, width)),) * 2,
        in_specs=[VMEM] * 10,
        out_specs=(VMEM,) * 3,
        scratch_shapes=[pltpu.VMEM((2, rows, 8 * width), BF16), pltpu.VMEM((12 * R, DE), BF16)],
        compiler_params=limit,
        cost_estimate=cost(32 * rows * width * width, 2**23),
    )(*near, w_query, w_out, w_key, w_value)
    token = partial[0, :1, :HDIM]
    far_a, far_b = after(far_a, token), after(far_b, token)
    fars = (far_a, far_b, across(far_a), across(far_b))
    query, grad_out, tails = pl.pallas_call(
        project_kernel,
        name="project",
        out_shape=(shape((rows, width)), shape((rows, width)), shape((2, CH, width))),
        in_specs=[VMEM] * 7,
        out_specs=(VMEM,) * 3,
        scratch_shapes=[pltpu.VMEM((rows, width), BF16)],
        compiler_params=limit,
        cost_estimate=cost(8 * rows * width * width, 2**23),
    )(*fars, w_query, w_out, partial)
    tails = along_ctx(tails, -1)
    positions, slots_of = spans * K * R, shape((4, CAP, R, DE))
    most = positions - K * R
    *last, away, own = pl.pallas_call(
        attend_kernel,
        name="attend",
        out_shape=(shape((K * R, width)), shape((K * R, width)), shape((rows - CH, width), F32))
        + (slots_of, slots_of),
        in_specs=[SMEM] + [VMEM] * 10,
        out_specs=(VMEM,) * 5,
        scratch_shapes=[
            pltpu.VMEM((4 * R, DE), BF16),
            pltpu.VMEM((4 * R, width), BF16),
            pltpu.VMEM((4 * R, width), BF16),
            pltpu.VMEM((positions, width), BF16),
            pltpu.VMEM((positions, width), BF16),
            pltpu.VMEM((most, width), BF16),
            pltpu.VMEM((most, width), BF16),
            pltpu.VMEM((most, DE), BF16),
        ],
        compiler_params=limit,
        cost_estimate=cost(8 * positions * DE * width, 2**23),
    )(shards, *fars, *near_states, w_key, w_value, query, grad_out)
    grad_query, away, own = pl.pallas_call(
        last_kernel,
        name="last",
        out_shape=(shape((rows, width)), slots_of, slots_of),
        in_specs=[SMEM] + [VMEM] * 8 + [VMEM] * 2,
        out_specs=(VMEM,) * 3,
        scratch_shapes=[
            pltpu.VMEM((K * R, width), BF16),
            pltpu.VMEM((K * R, width), BF16),
            pltpu.VMEM((K * R, DE), BF16),
        ],
        input_output_aliases={9: 1, 10: 2},
        compiler_params=limit,
        cost_estimate=cost(2 * positions * DE * width, 2**22),
    )(shards, query, grad_out, tails, last[0], last[1], w_key, w_value, last[2], away, own)
    got, half = across(away), CAP // 2
    far_up, far_down = far_sums(own, got, half)
    far_up, far_down = up(far_up.astype(BF16)), down(far_down.astype(BF16))
    nxt, prv = (x.astype(BF16) for x in near_sums(own, got, half, far_up, far_down))
    slots = add(own[0], got[0], up(nxt), down(prv)).astype(BF16)
    block = R // peers
    spread = slots.reshape(CAP, peers, block, DE).transpose(1, 0, 2, 3)
    labels = jnp.broadcast_to(label.astype(BF16), (peers,) + label.shape)
    spread = jnp.concatenate([spread, labels], -1)
    parts = lax.all_to_all(spread, "ctx", 0, 0, tiled=True)
    parts = parts.reshape(peers * CAP, block, DE + label.shape[-1])
    labels = parts[:, 0, DE].astype(jnp.int32)
    cross_away, cross_own = pl.pallas_call(
        cross_kernel,
        name="cross",
        out_shape=(shape((4, rows, width)), shape((4, rows, width))),
        in_specs=[VMEM] * 2,
        out_specs=(VMEM, VMEM),
        compiler_params=limit,
        cost_estimate=cost(2 * rows * width * 8 * width, 2**23),
    )(grad_query, w_query)
    cross_got, half = across(cross_away), rows // 2
    far_up, far_down = far_sums(cross_own, cross_got, half)
    far_up, far_down = up(far_up.astype(BF16)), down(far_down.astype(BF16))
    nxt, prv = near_sums(cross_own, cross_got, half, far_up, far_down)
    nxt, prv = nxt.astype(BF16), prv.astype(BF16)
    cross = add(cross_own[0], cross_got[0], up(nxt), down(prv))
    keep = rows - BORDER
    carried = along_ctx(cross[keep:].astype(BF16), 1).astype(F32)
    grad_states = cotangent.astype(F32) + jnp.concatenate([carried, cross[:keep]], 0)
    grad_database = pl.pallas_call(
        scatter_kernel,
        name="scatter",
        out_shape=shape((database.shape[0], block, DE), F32),
        in_specs=[SMEM, VMEM],
        out_specs=VMEM,
        compiler_params=limit,
        cost_estimate=cost(2**38, 2**32),
    )(labels, parts)
    return grad_states, grad_database


def solution(mesh):
    in_specs = (
        P("ctx", "db"),
        P("ctx", "db"),
        P(None, "db"),
        P(None, "db"),
        P(None, "db"),
        P("db", None),
        P("db", None, None),
        P("ctx", None),
        P("ctx", None),
    )
    out_specs = (P("ctx", "db"), P("db", "ctx", None))
    return jax.shard_map(
        per_device, mesh=mesh, in_specs=in_specs, out_specs=out_specs, check_vma=False
    )
```

```python
import functools

import jax
import jax.numpy as jnp
from jax import lax
from jax.experimental import pallas as pl
from jax.experimental.pallas import tpu as pltpu
from jax.sharding import PartitionSpec as P

HDIM = 128
DE = 896
CH = 64
R = 128
K = 2
CAP = 2
BORDER = CH - 1
SCALE = HDIM ** (-0.5)
BF16, F32 = jnp.bfloat16, jnp.float32
NT = (((1,), (1,)), ((), ()))
TN = (((0,), (0,)), ((), ()))
VMEM = pl.BlockSpec(memory_space=pltpu.VMEM)
SMEM = pl.BlockSpec(memory_space=pltpu.SMEM)
ANY = pl.BlockSpec(memory_space=pl.ANY)
HBM = pl.BlockSpec(memory_space=pltpu.HBM)


def up(x):
    return lax.ppermute(x, "db", [(s, (s + 2) % 8) for s in range(8)])


def down(x):
    return lax.ppermute(x, "db", [(s, (s - 2) % 8) for s in range(8)])


def across(x):
    return lax.ppermute(x, "db", [(s, s ^ 1) for s in range(8)])


def along_ctx(x, by):
    peers = lax.axis_size("ctx")
    return lax.ppermute(x, "ctx", [(i, i + by) for i in range(peers) if 0 <= i + by < peers])


def shape(dims, dtype=BF16):
    return jax.ShapeDtypeStruct(dims, dtype)


def cost(flops, size):
    return pl.CostEstimate(flops=flops, bytes_accessed=size, transcendentals=0)


def source_of(me, core, place):
    return lax.rem(me // 2 + place, 4) * 2 + (lax.rem(me, 2) + core) % 2


def named(shards, shard):
    count, found = jnp.int32(0), [jnp.int32(0)] * CAP
    for c in range(shards.shape[1]):
        for k in range(K):
            mine = shards[k, c] == shard
            for at in range(CAP):
                found[at] = jnp.where(mine & (count == at), c * K + k, found[at])
            count = count + mine.astype(jnp.int32)
    return found, count


def load_kernel(
    shard_ref, row_ref, states_ref, cotangent_ref, database_ref, a_ref, b_ref, label_ref, sems
):
    rows, width = states_ref.shape
    copies = []

    def copy(source, at, item, start, size):
        count = source.shape[-1] // HDIM
        for j in range(count):
            copies.append(
                pltpu.make_async_copy(
                    source.at[:, pl.ds(j * HDIM, HDIM)],
                    (a_ref, b_ref)[item].at[pl.ds(start + j * size, size)],
                    sems.at[at + j],
                )
            )
            copies[-1].start()

    copy(states_ref, 0, 0, 0, rows)
    copy(cotangent_ref, 4, 1, 0, rows)
    found, count = named(shard_ref, lax.axis_index("db"))
    named_rows = [row_ref[lax.rem(request, K), request // K] for request in found]
    for slot, row in enumerate(named_rows):
        copy(database_ref.at[row], 8 + 7 * slot, slot, rows * width // HDIM, R)
    for slot, row in enumerate(named_rows):
        label = jnp.where(count > slot, row, -1).astype(F32)
        label_ref[slot] = jnp.full(label_ref.shape[1:], label, F32)
    for each in copies:
        each.wait()


def hold_kernel(label_ref, a_ref, b_ref, a_out, b_out, done_ref, sems):
    copies = [
        pltpu.make_async_copy(src, dst, sems.at[at])
        for at, (src, dst) in enumerate(((a_ref, a_out), (b_ref, b_out)))
    ]
    for copy in copies:
        copy.start()
    for copy in copies:
        copy.wait()
    done_ref[...] = label_ref[...]


def near_kernel(*refs):
    blocks, weights, (wk_ref, wv_ref) = refs[:12], refs[12:14], refs[14:16]
    (sum_ref, k_ref, v_ref), (full, mem_s) = refs[16:19], refs[19:]
    me = lax.axis_index("db")
    rows, width = sum_ref.shape[1:]
    base = rows * width // HDIM
    for core in range(2):
        far = pl.multiple_of(source_of(me, core, 2) * width, width)
        full[:, :, pl.ds(far, width)] = jnp.zeros((2, rows, width), BF16)
        for at, place in enumerate((0, 1, 3)):
            spot = pl.multiple_of(source_of(me, core, place) * width, width)
            for item in range(2):
                block = blocks[core * 6 + at * 2 + item]
                for j in range(width // HDIM):
                    full[item, :, pl.ds(spot + j * HDIM, HDIM)] = block[pl.ds(j * rows, rows)]
                slot = ((core * 3 + at) * 2 + item) * R
                for j in range(DE // HDIM):
                    part = block[pl.ds(base + j * R, R)]
                    mem_s[pl.ds(slot, R), pl.ds(j * HDIM, HDIM)] = part
    sum_ref[0] = jnp.dot(full[0], weights[0][...], preferred_element_type=F32)
    sum_ref[1] = lax.dot_general(full[1], weights[1][...], NT, preferred_element_type=F32)
    k_ref[...] = jnp.dot(mem_s[...], wk_ref[...], preferred_element_type=F32).astype(BF16)
    v_ref[...] = jnp.dot(mem_s[...], wv_ref[...], preferred_element_type=F32).astype(BF16)


def project_kernel(*refs):
    fars, weights, sum_ref, outs, tail_ref, x_s = refs[:4], refs[4:6], refs[6], refs[7:9], *refs[9:]
    me = lax.axis_index("db")
    rows, width = outs[0].shape
    for item in range(2):
        total = sum_ref[item]
        for core in range(2):
            for j in range(width // HDIM):
                x_s[:, pl.ds(j * HDIM, HDIM)] = fars[core * 2 + item][pl.ds(j * rows, rows)]
            spot = pl.ds(pl.multiple_of(source_of(me, core, 2) * width, width), width)
            if item:
                part = lax.dot_general(
                    x_s[...], weights[1][:, spot], NT, preferred_element_type=F32
                )
            else:
                part = jnp.dot(x_s[...], weights[0][spot, :], preferred_element_type=F32)
            total = total + part
        total = pltpu.roll(total, rows - BORDER, 0).astype(BF16)
        outs[item][...] = total
        tail_ref[item] = total[rows - CH :]


def places_of(shard_ref):
    me = lax.axis_index("db")
    found = []
    for request in range(shard_ref.shape[1] * K):
        shard = shard_ref[request % K, request // K]
        rank = jnp.int32(0)
        for earlier in range(request):
            same = shard_ref[earlier % K, earlier // K] == shard
            rank = rank + same.astype(jnp.int32)
        core = (lax.rem(shard, 2) + lax.rem(me, 2)) % 2
        place = lax.rem(shard // 2 - me // 2 + 4, 4)
        found.append((core, place, jnp.minimum(rank, CAP - 1)))
    return found


def span_gradients(q, g, k_ref, v_ref, memory, gk_ref, gv_ref):
    some = range(len(q))
    at = [pl.ds(h * HDIM, HDIM) for h in some]
    k, v = [k_ref[memory, x] for x in at], [v_ref[memory, x] for x in at]
    scores = [lax.dot_general(q[h], k[h], NT, preferred_element_type=F32) * SCALE for h in some]
    dattention = [lax.dot_general(g[h], v[h], NT, preferred_element_type=F32) for h in some]
    raised = [jnp.exp(x - jnp.max(x, -1, keepdims=True)) for x in scores]
    attention = [x / jnp.sum(x, -1, keepdims=True) for x in raised]
    mean = [jnp.sum(attention[h] * dattention[h], -1, keepdims=True) for h in some]
    dscores = [(attention[h] * (dattention[h] - mean[h])).astype(BF16) for h in some]
    gq = [jnp.dot(dscores[h], k[h], preferred_element_type=F32) * SCALE for h in some]
    for h in some:
        gk = lax.dot_general(dscores[h], q[h], TN, preferred_element_type=F32) * SCALE
        gk_ref[memory, at[h]] = gk.astype(BF16)
    for h in some:
        gv = lax.dot_general(attention[h].astype(BF16), g[h], TN, preferred_element_type=F32)
        gv_ref[memory, at[h]] = gv.astype(BF16)
    return gq


def neighbour_terms(gk_ref, gv_ref, wk_ref, wv_ref, found, term_s, away_ref, own_ref):
    term = lax.dot_general(gk_ref[...], wk_ref[...], NT, preferred_element_type=F32)
    term = term + lax.dot_general(gv_ref[...], wv_ref[...], NT, preferred_element_type=F32)
    term_s[...] = term.astype(BF16)
    for at, (core, place, rank) in enumerate(found):
        spot = pl.ds(at * R, R)
        for which, ref in ((0, own_ref), (1, away_ref)):

            @pl.when(core == which)
            def _(spot=spot, place=place, rank=rank, ref=ref):
                ref[place, rank] = term_s[spot]


def attend_kernel(*refs):
    shard_ref, fars, k_near, v_near, wk_ref, wv_ref, q_ref, g_ref = refs[0], refs[1:5], *refs[5:11]
    k_ref, v_ref, gq_ref, away_ref, own_ref = refs[11:16]
    mem_s, k_far, v_far, k_s, v_s, gk_s, gv_s, term_s = refs[16:]
    rows, width = q_ref.shape
    spans = rows // CH
    base = rows * width // HDIM
    for slot, far in enumerate(fars):
        for j in range(DE // HDIM):
            part = far[pl.ds(base + j * R, R)]
            mem_s[pl.ds(slot * R, R), pl.ds(j * HDIM, HDIM)] = part
    k_far[...] = jnp.dot(mem_s[...], wk_ref[...], preferred_element_type=F32).astype(BF16)
    v_far[...] = jnp.dot(mem_s[...], wv_ref[...], preferred_element_type=F32).astype(BF16)
    found = places_of(shard_ref)
    for request, (core, place, rank) in enumerate(found):
        spot = pl.ds(request * R, R)

        @pl.when(place == 2)
        def _(spot=spot, slot=core * 2 + rank):
            source = pl.ds(pl.multiple_of(slot * R, R), R)
            k_s[spot], v_s[spot] = k_far[source], v_far[source]

        @pl.when(place != 2)
        def _(spot=spot, slot=(core * 3 + jnp.minimum(place, 2)) * 2 + rank):
            source = pl.ds(pl.multiple_of(slot * R, R), R)
            k_s[spot], v_s[spot] = k_near[source], v_near[source]

    heads = [pl.ds(h * HDIM, HDIM) for h in range(width // HDIM)]
    for c in range(spans - 1):
        span, memory = pl.ds(c * CH, CH), pl.ds(c * K * R, K * R)
        q, g = [q_ref[span, x] for x in heads], [g_ref[span, x] for x in heads]
        gq = span_gradients(q, g, k_s, v_s, memory, gk_s, gv_s)
        for x, value in zip(heads, gq):
            gq_ref[span, x] = value
    memory = pl.ds((spans - 1) * K * R, K * R)
    k_ref[...], v_ref[...] = k_s[memory], v_s[memory]
    first = found[: (spans - 1) * K]
    neighbour_terms(gk_s, gv_s, wk_ref, wv_ref, first, term_s, away_ref, own_ref)


def last_kernel(*refs):
    shard_ref, q_ref, g_ref, tail_ref, k_ref, v_ref, wk_ref, wv_ref, gq_in = refs[:9]
    gq_ref, away_ref, own_ref = refs[11:14]
    gk_s, gv_s, term_s = refs[14:]
    rows, width = q_ref.shape
    last = rows - CH
    heads = [pl.ds(h * HDIM, HDIM) for h in range(width // HDIM)]
    first_row = lax.broadcasted_iota(jnp.int32, (CH, HDIM), 0) == 0
    q, g = (
        [jnp.where(first_row, ref[last:, x], tail_ref[item, :, x]) for x in heads]
        for item, ref in enumerate((q_ref, g_ref))
    )
    gq = span_gradients(q, g, k_ref, v_ref, pl.ds(0, K * R), gk_s, gv_s)
    gq_ref[:last] = gq_in[...].astype(BF16)
    for x, value in zip(heads, gq):
        gq_ref[last:, x] = value.astype(BF16)
    found = places_of(shard_ref)[-K:]
    neighbour_terms(gk_s, gv_s, wk_ref, wv_ref, found, term_s, away_ref, own_ref)


def cross_kernel(gq_ref, w_ref, away_ref, own_ref):
    me = lax.axis_index("db")
    width = gq_ref.shape[1]
    for core, out in ((1, away_ref), (0, own_ref)):
        for place in range(4):
            spot = pl.multiple_of(source_of(me, core, place) * width, width)
            out[place] = lax.dot_general(
                gq_ref[...], w_ref[pl.ds(spot, width), :], NT, preferred_element_type=F32
            ).astype(BF16)


def scatter_kernel(label_ref, parts_ref, out_ref):
    out_ref[...] = jnp.zeros_like(out_ref)
    width = out_ref.shape[2]

    def item(i, carry):
        row = label_ref[i]

        @pl.when(row >= 0)
        def _():
            out_ref[row] += parts_ref[i][:, :width].astype(F32)

        return carry

    lax.fori_loop(0, parts_ref.shape[0], item, 0)


def after(x, token):
    return x + jnp.where(token > 0, -0.0, 0.0).astype(x.dtype)


def add(*parts):
    return functools.reduce(lambda a, b: a + b, [x.astype(F32) for x in parts])


def far_sums(own, got, half):
    return add(own[2][:half], got[2][:half]), add(own[2][half:], got[2][half:])


def near_sums(own, got, half, far_up, far_down):
    nxt = [add(own[1][:half], got[1][:half], far_up), add(own[1][half:], got[1][half:])]
    prv = [add(own[3][:half], got[3][:half]), add(own[3][half:], got[3][half:], far_down)]
    return jnp.concatenate(nxt, 0), jnp.concatenate(prv, 0)


def per_device(
    states, cotangent, w_query, w_key, w_value, w_out, database, neighbour_shard, neighbour_row
):
    rows, width = states.shape
    spans = rows // CH
    limit = pltpu.CompilerParams(vmem_limit_bytes=20 * 2**20)
    shards, named_rows = neighbour_shard.T, neighbour_row.T
    peers = lax.axis_size("ctx")

    given_rows = rows * width // HDIM + R * DE // HDIM
    *given, label = pl.pallas_call(
        load_kernel,
        name="load",
        out_shape=(shape((given_rows, HDIM)),) * 2 + (shape((CAP, 8, 128), F32),),
        in_specs=[SMEM, SMEM, ANY, ANY, ANY],
        out_specs=(VMEM,) * 3,
        scratch_shapes=[pltpu.SemaphoreType.DMA((2 * (width + DE) // HDIM,))],
    )(shards, named_rows, states, cotangent, database)
    *held, done = pl.pallas_call(
        hold_kernel,
        name="hold",
        out_shape=(shape(w_query.shape), shape(w_out.shape), shape(label.shape, F32)),
        in_specs=[VMEM, HBM, HBM],
        out_specs=(VMEM,) * 3,
        scratch_shapes=[pltpu.SemaphoreType.DMA((2,))],
        compiler_params=limit,
    )(label, w_query, w_out)
    prv_a, nxt_b = up(given[0]), down(given[1])
    prv_b, nxt_a = up(given[1]), down(given[0])
    token = done[0, :1]
    far_a, far_b = up(after(prv_a, token)), down(after(nxt_b, token))
    near = (*given, nxt_a, nxt_b, prv_a, prv_b)
    near = near + tuple(across(x) for x in given)
    near = near + (across(after(nxt_a, token)), across(after(nxt_b, prv_b[:1])))
    near = near + (across(after(prv_a, nxt_a[:1])), across(after(prv_b, token)))
    partial, *near_states = pl.pallas_call(
        near_kernel,
        name="near",
        out_shape=(shape((2, rows, width), F32),) + (shape((12 * R, width)),) * 2,
        in_specs=[VMEM] * 16,
        out_specs=(VMEM,) * 3,
        scratch_shapes=[pltpu.VMEM((2, rows, 8 * width), BF16), pltpu.VMEM((12 * R, DE), BF16)],
        compiler_params=limit,
        cost_estimate=cost(1, 1),
    )(*near, *held, w_key, w_value)
    token = partial[0, :1, :HDIM]
    far_a, far_b = after(far_a, token), after(far_b, token)
    fars = (far_a, far_b, across(far_a), across(far_b))
    query, grad_out, tails = pl.pallas_call(
        project_kernel,
        name="project",
        out_shape=(shape((rows, width)), shape((rows, width)), shape((2, CH, width))),
        in_specs=[VMEM] * 7,
        out_specs=(VMEM,) * 3,
        scratch_shapes=[pltpu.VMEM((rows, width), BF16)],
        compiler_params=limit,
        cost_estimate=cost(8 * rows * width * width, 2**23),
    )(*fars, *held, partial)
    tails = along_ctx(tails, -1)
    positions, slots_of = spans * K * R, shape((4, CAP, R, DE))
    most = positions - K * R
    *last, away, own = pl.pallas_call(
        attend_kernel,
        name="attend",
        out_shape=(shape((K * R, width)), shape((K * R, width)), shape((rows - CH, width), F32))
        + (slots_of, slots_of),
        in_specs=[SMEM] + [VMEM] * 10,
        out_specs=(VMEM,) * 5,
        scratch_shapes=[
            pltpu.VMEM((4 * R, DE), BF16),
            pltpu.VMEM((4 * R, width), BF16),
            pltpu.VMEM((4 * R, width), BF16),
            pltpu.VMEM((positions, width), BF16),
            pltpu.VMEM((positions, width), BF16),
            pltpu.VMEM((most, width), BF16),
            pltpu.VMEM((most, width), BF16),
            pltpu.VMEM((most, DE), BF16),
        ],
        compiler_params=limit,
        cost_estimate=cost(8 * positions * DE * width, 2**23),
    )(shards, *fars, *near_states, w_key, w_value, query, grad_out)
    grad_query, away, own = pl.pallas_call(
        last_kernel,
        name="last",
        out_shape=(shape((rows, width)), slots_of, slots_of),
        in_specs=[SMEM] + [VMEM] * 8 + [VMEM] * 2,
        out_specs=(VMEM,) * 3,
        scratch_shapes=[
            pltpu.VMEM((K * R, width), BF16),
            pltpu.VMEM((K * R, width), BF16),
            pltpu.VMEM((K * R, DE), BF16),
        ],
        input_output_aliases={9: 1, 10: 2},
        compiler_params=limit,
        cost_estimate=cost(2 * positions * DE * width, 2**22),
    )(shards, query, grad_out, tails, last[0], last[1], w_key, w_value, last[2], away, own)
    got, half = across(away), CAP // 2
    far_up, far_down = far_sums(own, got, half)
    far_up, far_down = up(far_up.astype(BF16)), down(far_down.astype(BF16))
    nxt, prv = (x.astype(BF16) for x in near_sums(own, got, half, far_up, far_down))
    slots = add(own[0], got[0], up(nxt), down(prv)).astype(BF16)
    block = R // peers
    spread = slots.reshape(CAP, peers, block, DE).transpose(1, 0, 2, 3)
    labels = jnp.broadcast_to(label.astype(BF16), (peers,) + label.shape)
    spread = jnp.concatenate([spread, labels], -1)
    parts = lax.all_to_all(spread, "ctx", 0, 0, tiled=True)
    parts = parts.reshape(peers * CAP, block, DE + label.shape[-1])
    labels = parts[:, 0, DE].astype(jnp.int32)
    cross_away, cross_own = pl.pallas_call(
        cross_kernel,
        name="cross",
        out_shape=(shape((4, rows, width)), shape((4, rows, width))),
        in_specs=[VMEM] * 2,
        out_specs=(VMEM, VMEM),
        compiler_params=limit,
        cost_estimate=cost(2 * rows * width * 8 * width, 2**23),
    )(grad_query, held[0])
    cross_got, half = across(cross_away), rows // 2
    far_up, far_down = far_sums(cross_own, cross_got, half)
    far_up, far_down = up(far_up.astype(BF16)), down(far_down.astype(BF16))
    nxt, prv = near_sums(cross_own, cross_got, half, far_up, far_down)
    nxt, prv = nxt.astype(BF16), prv.astype(BF16)
    cross = add(cross_own[0], cross_got[0], up(nxt), down(prv))
    keep = rows - BORDER
    carried = along_ctx(cross[keep:].astype(BF16), 1).astype(F32)
    grad_states = cotangent.astype(F32) + jnp.concatenate([carried, cross[:keep]], 0)
    grad_database = pl.pallas_call(
        scatter_kernel,
        name="scatter",
        out_shape=shape((database.shape[0], block, DE), F32),
        in_specs=[SMEM, VMEM],
        out_specs=VMEM,
        compiler_params=limit,
        cost_estimate=cost(2**38, 2**32),
    )(labels, parts)
    return grad_states, grad_database


def solution(mesh):
    in_specs = (
        P("ctx", "db"),
        P("ctx", "db"),
        P(None, "db"),
        P(None, "db"),
        P(None, "db"),
        P("db", None),
        P("db", None, None),
        P("ctx", None),
        P("ctx", None),
    )
    out_specs = (P("ctx", "db"), P("db", "ctx", None))
    return jax.shard_map(
        per_device, mesh=mesh, in_specs=in_specs, out_specs=out_specs, check_vma=False
    )
```

```python
import functools

import jax
import jax.numpy as jnp
from jax import lax
from jax.experimental import pallas as pl
from jax.experimental.pallas import tpu as pltpu
from jax.sharding import PartitionSpec as P

HDIM = 128
DE = 896
CH = 64
R = 128
K = 2
CAP = 2
BORDER = CH - 1
SCALE = HDIM ** (-0.5)
BF16, F32 = jnp.bfloat16, jnp.float32
NT = (((1,), (1,)), ((), ()))
TN = (((0,), (0,)), ((), ()))
VMEM = pl.BlockSpec(memory_space=pltpu.VMEM)
SMEM = pl.BlockSpec(memory_space=pltpu.SMEM)
ANY = pl.BlockSpec(memory_space=pl.ANY)
HBM = pl.BlockSpec(memory_space=pltpu.HBM)


def up(x):
    return lax.ppermute(x, "db", [(s, (s + 2) % 8) for s in range(8)])


def down(x):
    return lax.ppermute(x, "db", [(s, (s - 2) % 8) for s in range(8)])


def across(x):
    return lax.ppermute(x, "db", [(s, s ^ 1) for s in range(8)])


def along_ctx(x, by):
    peers = lax.axis_size("ctx")
    return lax.ppermute(x, "ctx", [(i, i + by) for i in range(peers) if 0 <= i + by < peers])


def shape(dims, dtype=BF16):
    return jax.ShapeDtypeStruct(dims, dtype)


def cost(flops, size):
    return pl.CostEstimate(flops=flops, bytes_accessed=size, transcendentals=0)


def source_of(me, core, place):
    return lax.rem(me // 2 + place, 4) * 2 + (lax.rem(me, 2) + core) % 2


def named(shards, shard):
    count, found = jnp.int32(0), [jnp.int32(0)] * CAP
    for c in range(shards.shape[1]):
        for k in range(K):
            mine = shards[k, c] == shard
            for at in range(CAP):
                found[at] = jnp.where(mine & (count == at), c * K + k, found[at])
            count = count + mine.astype(jnp.int32)
    return found, count


def load_kernel(
    shard_ref, row_ref, states_ref, cotangent_ref, database_ref, a_ref, b_ref, label_ref, sems
):
    rows, width = states_ref.shape
    copies = []

    def copy(source, at, item, start, size):
        count = source.shape[-1] // HDIM
        for j in range(count):
            copies.append(
                pltpu.make_async_copy(
                    source.at[:, pl.ds(j * HDIM, HDIM)],
                    (a_ref, b_ref)[item].at[pl.ds(start + j * size, size)],
                    sems.at[at + j],
                )
            )
            copies[-1].start()

    copy(states_ref, 0, 0, 0, rows)
    copy(cotangent_ref, 4, 1, 0, rows)
    found, count = named(shard_ref, lax.axis_index("db"))
    named_rows = [row_ref[lax.rem(request, K), request // K] for request in found]
    for slot, row in enumerate(named_rows):
        copy(database_ref.at[row], 8 + 7 * slot, slot, rows * width // HDIM, R)
    for slot, row in enumerate(named_rows):
        label = jnp.where(count > slot, row, -1).astype(F32)
        label_ref[slot] = jnp.full(label_ref.shape[1:], label, F32)
    for each in copies:
        each.wait()


def hold_kernel(label_ref, a_ref, b_ref, a_out, b_out, done_ref, sems):
    copies = [
        pltpu.make_async_copy(src, dst, sems.at[at])
        for at, (src, dst) in enumerate(((a_ref, a_out), (b_ref, b_out)))
    ]
    for copy in copies:
        copy.start()
    for copy in copies:
        copy.wait()
    done_ref[...] = label_ref[...]


def near_kernel(*refs):
    blocks, weights, (wk_ref, wv_ref) = refs[:12], refs[12:14], refs[14:16]
    (sum_ref, k_ref, v_ref), (full, mem_s) = refs[16:19], refs[19:]
    me = lax.axis_index("db")
    rows, width = sum_ref.shape[1:]
    base = rows * width // HDIM
    for core in range(2):
        far = pl.multiple_of(source_of(me, core, 2) * width, width)
        full[:, :, pl.ds(far, width)] = jnp.zeros((2, rows, width), BF16)
        for at, place in enumerate((0, 1, 3)):
            spot = pl.multiple_of(source_of(me, core, place) * width, width)
            for item in range(2):
                block = blocks[core * 6 + at * 2 + item]
                for j in range(width // HDIM):
                    full[item, :, pl.ds(spot + j * HDIM, HDIM)] = block[pl.ds(j * rows, rows)]
                slot = ((core * 3 + at) * 2 + item) * R
                for j in range(DE // HDIM):
                    part = block[pl.ds(base + j * R, R)]
                    mem_s[pl.ds(slot, R), pl.ds(j * HDIM, HDIM)] = part
    sum_ref[0] = jnp.dot(full[0], weights[0][...], preferred_element_type=F32)
    sum_ref[1] = lax.dot_general(full[1], weights[1][...], NT, preferred_element_type=F32)
    k_ref[...] = jnp.dot(mem_s[...], wk_ref[...], preferred_element_type=F32).astype(BF16)
    v_ref[...] = jnp.dot(mem_s[...], wv_ref[...], preferred_element_type=F32).astype(BF16)


def project_kernel(*refs):
    fars, weights, sum_ref, outs, tail_ref, x_s = refs[:4], refs[4:6], refs[6], refs[7:9], *refs[9:]
    me = lax.axis_index("db")
    rows, width = outs[0].shape
    for item in range(2):
        total = sum_ref[item]
        for core in range(2):
            for j in range(width // HDIM):
                x_s[:, pl.ds(j * HDIM, HDIM)] = fars[core * 2 + item][pl.ds(j * rows, rows)]
            spot = pl.ds(pl.multiple_of(source_of(me, core, 2) * width, width), width)
            if item:
                part = lax.dot_general(
                    x_s[...], weights[1][:, spot], NT, preferred_element_type=F32
                )
            else:
                part = jnp.dot(x_s[...], weights[0][spot, :], preferred_element_type=F32)
            total = total + part
        total = pltpu.roll(total, rows - BORDER, 0).astype(BF16)
        outs[item][...] = total
        tail_ref[item] = total[rows - CH :]


def places_of(shard_ref):
    me = lax.axis_index("db")
    found = []
    for request in range(shard_ref.shape[1] * K):
        shard = shard_ref[request % K, request // K]
        rank = jnp.int32(0)
        for earlier in range(request):
            same = shard_ref[earlier % K, earlier // K] == shard
            rank = rank + same.astype(jnp.int32)
        core = (lax.rem(shard, 2) + lax.rem(me, 2)) % 2
        place = lax.rem(shard // 2 - me // 2 + 4, 4)
        found.append((core, place, jnp.minimum(rank, CAP - 1)))
    return found


def span_gradients(q, g, k_ref, v_ref, memory, gk_ref, gv_ref):
    some = range(len(q))
    at = [pl.ds(h * HDIM, HDIM) for h in some]
    k, v = [k_ref[memory, x] for x in at], [v_ref[memory, x] for x in at]
    scores = [lax.dot_general(q[h], k[h], NT, preferred_element_type=F32) * SCALE for h in some]
    dattention = [lax.dot_general(g[h], v[h], NT, preferred_element_type=F32) for h in some]
    raised = [jnp.exp(x - jnp.max(x, -1, keepdims=True)) for x in scores]
    attention = [x / jnp.sum(x, -1, keepdims=True) for x in raised]
    mean = [jnp.sum(attention[h] * dattention[h], -1, keepdims=True) for h in some]
    dscores = [(attention[h] * (dattention[h] - mean[h])).astype(BF16) for h in some]
    gq = [jnp.dot(dscores[h], k[h], preferred_element_type=F32) * SCALE for h in some]
    for h in some:
        gk = lax.dot_general(dscores[h], q[h], TN, preferred_element_type=F32) * SCALE
        gk_ref[memory, at[h]] = gk.astype(BF16)
    for h in some:
        gv = lax.dot_general(attention[h].astype(BF16), g[h], TN, preferred_element_type=F32)
        gv_ref[memory, at[h]] = gv.astype(BF16)
    return gq


def neighbour_terms(gk_ref, gv_ref, wk_ref, wv_ref, found, term_s, away_ref, own_ref):
    term = lax.dot_general(gk_ref[...], wk_ref[...], NT, preferred_element_type=F32)
    term = term + lax.dot_general(gv_ref[...], wv_ref[...], NT, preferred_element_type=F32)
    term_s[...] = term.astype(BF16)
    for at, (core, place, rank) in enumerate(found):
        spot = pl.ds(at * R, R)
        for which, ref in ((0, own_ref), (1, away_ref)):

            @pl.when(core == which)
            def _(spot=spot, place=place, rank=rank, ref=ref):
                ref[place, rank] = term_s[spot]


def attend_kernel(*refs):
    shard_ref, fars, k_near, v_near, wk_ref, wv_ref, q_ref, g_ref = refs[0], refs[1:5], *refs[5:11]
    k_ref, v_ref, gq_ref, away_ref, own_ref = refs[11:16]
    mem_s, k_far, v_far, k_s, v_s, gk_s, gv_s, term_s = refs[16:]
    rows, width = q_ref.shape
    spans = rows // CH
    base = rows * width // HDIM
    for slot, far in enumerate(fars):
        for j in range(DE // HDIM):
            part = far[pl.ds(base + j * R, R)]
            mem_s[pl.ds(slot * R, R), pl.ds(j * HDIM, HDIM)] = part
    k_far[...] = jnp.dot(mem_s[...], wk_ref[...], preferred_element_type=F32).astype(BF16)
    v_far[...] = jnp.dot(mem_s[...], wv_ref[...], preferred_element_type=F32).astype(BF16)
    found = places_of(shard_ref)
    for request, (core, place, rank) in enumerate(found):
        spot = pl.ds(request * R, R)

        @pl.when(place == 2)
        def _(spot=spot, slot=core * 2 + rank):
            source = pl.ds(pl.multiple_of(slot * R, R), R)
            k_s[spot], v_s[spot] = k_far[source], v_far[source]

        @pl.when(place != 2)
        def _(spot=spot, slot=(core * 3 + jnp.minimum(place, 2)) * 2 + rank):
            source = pl.ds(pl.multiple_of(slot * R, R), R)
            k_s[spot], v_s[spot] = k_near[source], v_near[source]

    heads = [pl.ds(h * HDIM, HDIM) for h in range(width // HDIM)]
    for c in range(spans - 1):
        span, memory = pl.ds(c * CH, CH), pl.ds(c * K * R, K * R)
        q, g = [q_ref[span, x] for x in heads], [g_ref[span, x] for x in heads]
        gq = span_gradients(q, g, k_s, v_s, memory, gk_s, gv_s)
        for x, value in zip(heads, gq):
            gq_ref[span, x] = value
    memory = pl.ds((spans - 1) * K * R, K * R)
    k_ref[...], v_ref[...] = k_s[memory], v_s[memory]
    first = found[: (spans - 1) * K]
    neighbour_terms(gk_s, gv_s, wk_ref, wv_ref, first, term_s, away_ref, own_ref)


def last_kernel(*refs):
    shard_ref, q_ref, g_ref, tail_ref, k_ref, v_ref, wk_ref, wv_ref, gq_in = refs[:9]
    gq_ref, away_ref, own_ref = refs[11:14]
    gk_s, gv_s, term_s = refs[14:]
    rows, width = q_ref.shape
    last = rows - CH
    heads = [pl.ds(h * HDIM, HDIM) for h in range(width // HDIM)]
    first_row = lax.broadcasted_iota(jnp.int32, (CH, HDIM), 0) == 0
    q, g = (
        [jnp.where(first_row, ref[last:, x], tail_ref[item, :, x]) for x in heads]
        for item, ref in enumerate((q_ref, g_ref))
    )
    gq = span_gradients(q, g, k_ref, v_ref, pl.ds(0, K * R), gk_s, gv_s)
    gq_ref[:last] = gq_in[...].astype(BF16)
    for x, value in zip(heads, gq):
        gq_ref[last:, x] = value.astype(BF16)
    found = places_of(shard_ref)[-K:]
    neighbour_terms(gk_s, gv_s, wk_ref, wv_ref, found, term_s, away_ref, own_ref)


def cross_kernel(gq_ref, w_ref, away_ref, own_ref):
    me = lax.axis_index("db")
    width = gq_ref.shape[1]
    for core, out in ((1, away_ref), (0, own_ref)):
        for place in range(4):
            spot = pl.multiple_of(source_of(me, core, place) * width, width)
            out[place] = lax.dot_general(
                gq_ref[...], w_ref[pl.ds(spot, width), :], NT, preferred_element_type=F32
            ).astype(BF16)


def scatter_kernel(label_ref, parts_ref, out_ref):
    out_ref[...] = jnp.zeros_like(out_ref)
    width = out_ref.shape[2]

    for i in range(parts_ref.shape[0]):
        row = label_ref[i]

        @pl.when(row >= 0)
        def _(i=i, row=row):
            out_ref[row] += parts_ref[i][:, :width].astype(F32)


def after(x, token):
    return x + jnp.where(token > 0, -0.0, 0.0).astype(x.dtype)


def add(*parts):
    return functools.reduce(lambda a, b: a + b, [x.astype(F32) for x in parts])


def far_sums(own, got, half):
    return add(own[2][:half], got[2][:half]), add(own[2][half:], got[2][half:])


def near_sums(own, got, half, far_up, far_down):
    nxt = [add(own[1][:half], got[1][:half], far_up), add(own[1][half:], got[1][half:])]
    prv = [add(own[3][:half], got[3][:half]), add(own[3][half:], got[3][half:], far_down)]
    return jnp.concatenate(nxt, 0), jnp.concatenate(prv, 0)


def per_device(
    states, cotangent, w_query, w_key, w_value, w_out, database, neighbour_shard, neighbour_row
):
    rows, width = states.shape
    spans = rows // CH
    limit = pltpu.CompilerParams(vmem_limit_bytes=20 * 2**20)
    shards, named_rows = neighbour_shard.T, neighbour_row.T
    peers = lax.axis_size("ctx")

    given_rows = rows * width // HDIM + R * DE // HDIM
    *given, label = pl.pallas_call(
        load_kernel,
        name="load",
        out_shape=(shape((given_rows, HDIM)),) * 2 + (shape((CAP, 8, 128), F32),),
        in_specs=[SMEM, SMEM, ANY, ANY, ANY],
        out_specs=(VMEM,) * 3,
        scratch_shapes=[pltpu.SemaphoreType.DMA((2 * (width + DE) // HDIM,))],
    )(shards, named_rows, states, cotangent, database)
    *held, done = pl.pallas_call(
        hold_kernel,
        name="hold",
        out_shape=(shape(w_query.shape), shape(w_out.shape), shape(label.shape, F32)),
        in_specs=[VMEM, HBM, HBM],
        out_specs=(VMEM,) * 3,
        scratch_shapes=[pltpu.SemaphoreType.DMA((2,))],
        compiler_params=limit,
    )(label, w_query, w_out)
    prv_a, nxt_b = up(given[0]), down(given[1])
    prv_b, nxt_a = up(given[1]), down(given[0])
    token = done[0, :1]
    far_a, far_b = up(after(prv_a, token)), down(after(nxt_b, token))
    near = (*given, nxt_a, nxt_b, prv_a, prv_b)
    near = near + tuple(across(x) for x in given)
    near = near + (across(after(nxt_a, token)), across(after(nxt_b, prv_b[:1])))
    near = near + (across(after(prv_a, nxt_a[:1])), across(after(prv_b, token)))
    partial, *near_states = pl.pallas_call(
        near_kernel,
        name="near",
        out_shape=(shape((2, rows, width), F32),) + (shape((12 * R, width)),) * 2,
        in_specs=[VMEM] * 16,
        out_specs=(VMEM,) * 3,
        scratch_shapes=[pltpu.VMEM((2, rows, 8 * width), BF16), pltpu.VMEM((12 * R, DE), BF16)],
        compiler_params=limit,
        cost_estimate=cost(1, 1),
    )(*near, *held, w_key, w_value)
    token = partial[0, :1, :HDIM]
    far_a, far_b = after(far_a, token), after(far_b, token)
    fars = (far_a, far_b, across(far_a), across(far_b))
    query, grad_out, tails = pl.pallas_call(
        project_kernel,
        name="project",
        out_shape=(shape((rows, width)), shape((rows, width)), shape((2, CH, width))),
        in_specs=[VMEM] * 7,
        out_specs=(VMEM,) * 3,
        scratch_shapes=[pltpu.VMEM((rows, width), BF16)],
        compiler_params=limit,
        cost_estimate=cost(8 * rows * width * width, 2**23),
    )(*fars, *held, partial)
    tails = along_ctx(tails, -1)
    positions, slots_of = spans * K * R, shape((4, CAP, R, DE))
    most = positions - K * R
    *last, away, own = pl.pallas_call(
        attend_kernel,
        name="attend",
        out_shape=(shape((K * R, width)), shape((K * R, width)), shape((rows - CH, width), F32))
        + (slots_of, slots_of),
        in_specs=[SMEM] + [VMEM] * 10,
        out_specs=(VMEM,) * 5,
        scratch_shapes=[
            pltpu.VMEM((4 * R, DE), BF16),
            pltpu.VMEM((4 * R, width), BF16),
            pltpu.VMEM((4 * R, width), BF16),
            pltpu.VMEM((positions, width), BF16),
            pltpu.VMEM((positions, width), BF16),
            pltpu.VMEM((most, width), BF16),
            pltpu.VMEM((most, width), BF16),
            pltpu.VMEM((most, DE), BF16),
        ],
        compiler_params=limit,
        cost_estimate=cost(8 * positions * DE * width, 2**23),
    )(shards, *fars, *near_states, w_key, w_value, query, grad_out)
    grad_query, away, own = pl.pallas_call(
        last_kernel,
        name="last",
        out_shape=(shape((rows, width)), slots_of, slots_of),
        in_specs=[SMEM] + [VMEM] * 8 + [VMEM] * 2,
        out_specs=(VMEM,) * 3,
        scratch_shapes=[
            pltpu.VMEM((K * R, width), BF16),
            pltpu.VMEM((K * R, width), BF16),
            pltpu.VMEM((K * R, DE), BF16),
        ],
        input_output_aliases={9: 1, 10: 2},
        compiler_params=limit,
        cost_estimate=cost(2 * positions * DE * width, 2**22),
    )(shards, query, grad_out, tails, last[0], last[1], w_key, w_value, last[2], away, own)
    got, half = across(away), CAP // 2
    far_up, far_down = far_sums(own, got, half)
    far_up, far_down = up(far_up.astype(BF16)), down(far_down.astype(BF16))
    nxt, prv = (x.astype(BF16) for x in near_sums(own, got, half, far_up, far_down))
    slots = add(own[0], got[0], up(nxt), down(prv)).astype(BF16)
    block = R // peers
    spread = slots.reshape(CAP, peers, block, DE).transpose(1, 0, 2, 3)
    labels = jnp.broadcast_to(label.astype(BF16), (peers,) + label.shape)
    spread = jnp.concatenate([spread, labels], -1)
    parts = lax.all_to_all(spread, "ctx", 0, 0, tiled=True)
    parts = parts.reshape(peers * CAP, block, DE + label.shape[-1])
    labels = parts[:, 0, DE].astype(jnp.int32)
    cross_away, cross_own = pl.pallas_call(
        cross_kernel,
        name="cross",
        out_shape=(shape((4, rows, width)), shape((4, rows, width))),
        in_specs=[VMEM] * 2,
        out_specs=(VMEM, VMEM),
        compiler_params=limit,
        cost_estimate=cost(2 * rows * width * 8 * width, 2**23),
    )(grad_query, held[0])
    cross_got, half = across(cross_away), rows // 2
    far_up, far_down = far_sums(cross_own, cross_got, half)
    far_up, far_down = up(far_up.astype(BF16)), down(far_down.astype(BF16))
    nxt, prv = near_sums(cross_own, cross_got, half, far_up, far_down)
    nxt, prv = nxt.astype(BF16), prv.astype(BF16)
    cross = add(cross_own[0], cross_got[0], up(nxt), down(prv))
    keep = rows - BORDER
    carried = along_ctx(cross[keep:].astype(BF16), 1).astype(F32)
    grad_states = cotangent.astype(F32) + jnp.concatenate([carried, cross[:keep]], 0)
    grad_database = pl.pallas_call(
        scatter_kernel,
        name="scatter",
        out_shape=shape((database.shape[0], block, DE), F32),
        in_specs=[SMEM, VMEM],
        out_specs=VMEM,
        compiler_params=limit,
        cost_estimate=cost(2**38, 2**32),
    )(labels, parts)
    return grad_states, grad_database


def solution(mesh):
    in_specs = (
        P("ctx", "db"),
        P("ctx", "db"),
        P(None, "db"),
        P(None, "db"),
        P(None, "db"),
        P("db", None),
        P("db", None, None),
        P("ctx", None),
        P("ctx", None),
    )
    out_specs = (P("ctx", "db"), P("db", "ctx", None))
    return jax.shard_map(
        per_device, mesh=mesh, in_specs=in_specs, out_specs=out_specs, check_vma=False
    )
```

```python
import functools

import jax
import jax.numpy as jnp
from jax import lax
from jax.experimental import pallas as pl
from jax.experimental.pallas import tpu as pltpu
from jax.sharding import PartitionSpec as P

HDIM = 128
DE = 896
CH = 64
R = 128
K = 2
CAP = 2
BORDER = CH - 1
SCALE = HDIM ** (-0.5)
BF16, F32 = jnp.bfloat16, jnp.float32
NT = (((1,), (1,)), ((), ()))
TN = (((0,), (0,)), ((), ()))
VMEM = pl.BlockSpec(memory_space=pltpu.VMEM)
SMEM = pl.BlockSpec(memory_space=pltpu.SMEM)
ANY = pl.BlockSpec(memory_space=pl.ANY)
HBM = pl.BlockSpec(memory_space=pltpu.HBM)


def up(x):
    return lax.ppermute(x, "db", [(s, (s + 2) % 8) for s in range(8)])


def down(x):
    return lax.ppermute(x, "db", [(s, (s - 2) % 8) for s in range(8)])


def across(x):
    return lax.ppermute(x, "db", [(s, s ^ 1) for s in range(8)])


def along_ctx(x, by):
    peers = lax.axis_size("ctx")
    return lax.ppermute(x, "ctx", [(i, i + by) for i in range(peers) if 0 <= i + by < peers])


def shape(dims, dtype=BF16):
    return jax.ShapeDtypeStruct(dims, dtype)


def cost(flops, size):
    return pl.CostEstimate(flops=flops, bytes_accessed=size, transcendentals=0)


def source_of(me, core, place):
    return lax.rem(me // 2 + place, 4) * 2 + (lax.rem(me, 2) + core) % 2


def named(shards, shard):
    count, found = jnp.int32(0), [jnp.int32(0)] * CAP
    for c in range(shards.shape[1]):
        for k in range(K):
            mine = shards[k, c] == shard
            for at in range(CAP):
                found[at] = jnp.where(mine & (count == at), c * K + k, found[at])
            count = count + mine.astype(jnp.int32)
    return found, count


def load_kernel(
    shard_ref, row_ref, states_ref, cotangent_ref, database_ref, a_ref, b_ref, label_ref, sems
):
    rows, width = states_ref.shape
    copies = []

    def copy(source, at, item, start, size):
        count = source.shape[-1] // HDIM
        for j in range(count):
            copies.append(
                pltpu.make_async_copy(
                    source.at[:, pl.ds(j * HDIM, HDIM)],
                    (a_ref, b_ref)[item].at[pl.ds(start + j * size, size)],
                    sems.at[at + j],
                )
            )
            copies[-1].start()

    copy(states_ref, 0, 0, 0, rows)
    copy(cotangent_ref, 4, 1, 0, rows)
    found, count = named(shard_ref, lax.axis_index("db"))
    named_rows = [row_ref[lax.rem(request, K), request // K] for request in found]
    for slot, row in enumerate(named_rows):
        copy(database_ref.at[row], 8 + 7 * slot, slot, rows * width // HDIM, R)
    for slot, row in enumerate(named_rows):
        label = jnp.where(count > slot, row, -1).astype(F32)
        label_ref[slot] = jnp.full(label_ref.shape[1:], label, F32)
    for each in copies:
        each.wait()


def hold_kernel(label_ref, a_ref, b_ref, a_out, b_out, done_ref, sems):
    copies = [
        pltpu.make_async_copy(src, dst, sems.at[at])
        for at, (src, dst) in enumerate(((a_ref, a_out), (b_ref, b_out)))
    ]
    for copy in copies:
        copy.start()
    for copy in copies:
        copy.wait()
    done_ref[...] = label_ref[...]


def near_kernel(*refs):
    blocks, weights, (wk_ref, wv_ref) = refs[:12], refs[12:14], refs[14:16]
    (sum_ref, k_ref, v_ref), (full, mem_s) = refs[16:19], refs[19:]
    me = lax.axis_index("db")
    rows, width = sum_ref.shape[1:]
    base = rows * width // HDIM
    for core in range(2):
        far = pl.multiple_of(source_of(me, core, 2) * width, width)
        full[:, :, pl.ds(far, width)] = jnp.zeros((2, rows, width), BF16)
        for at, place in enumerate((0, 1, 3)):
            spot = pl.multiple_of(source_of(me, core, place) * width, width)
            for item in range(2):
                block = blocks[core * 6 + at * 2 + item]
                for j in range(width // HDIM):
                    full[item, :, pl.ds(spot + j * HDIM, HDIM)] = block[pl.ds(j * rows, rows)]
                slot = ((core * 3 + at) * 2 + item) * R
                for j in range(DE // HDIM):
                    part = block[pl.ds(base + j * R, R)]
                    mem_s[pl.ds(slot, R), pl.ds(j * HDIM, HDIM)] = part
    sum_ref[0] = jnp.dot(full[0], weights[0][...], preferred_element_type=F32)
    sum_ref[1] = lax.dot_general(full[1], weights[1][...], NT, preferred_element_type=F32)
    k_ref[...] = jnp.dot(mem_s[...], wk_ref[...], preferred_element_type=F32).astype(BF16)
    v_ref[...] = jnp.dot(mem_s[...], wv_ref[...], preferred_element_type=F32).astype(BF16)


def project_kernel(*refs):
    fars, weights, sum_ref, outs, tail_ref, x_s = refs[:4], refs[4:6], refs[6], refs[7:9], *refs[9:]
    me = lax.axis_index("db")
    rows, width = outs[0].shape
    for item in range(2):
        total = sum_ref[item]
        for core in range(2):
            for j in range(width // HDIM):
                x_s[:, pl.ds(j * HDIM, HDIM)] = fars[core * 2 + item][pl.ds(j * rows, rows)]
            spot = pl.ds(pl.multiple_of(source_of(me, core, 2) * width, width), width)
            if item:
                part = lax.dot_general(
                    x_s[...], weights[1][:, spot], NT, preferred_element_type=F32
                )
            else:
                part = jnp.dot(x_s[...], weights[0][spot, :], preferred_element_type=F32)
            total = total + part
        total = pltpu.roll(total, rows - BORDER, 0).astype(BF16)
        outs[item][...] = total
        tail_ref[item] = total[rows - CH :]


def places_of(shard_ref):
    me = lax.axis_index("db")
    found = []
    for request in range(shard_ref.shape[1] * K):
        shard = shard_ref[request % K, request // K]
        rank = jnp.int32(0)
        for earlier in range(request):
            same = shard_ref[earlier % K, earlier // K] == shard
            rank = rank + same.astype(jnp.int32)
        core = (lax.rem(shard, 2) + lax.rem(me, 2)) % 2
        place = lax.rem(shard // 2 - me // 2 + 4, 4)
        found.append((core, place, jnp.minimum(rank, CAP - 1)))
    return found


def span_gradients(q, g, k_ref, v_ref, memory, gk_ref, gv_ref):
    some = range(len(q))
    at = [pl.ds(h * HDIM, HDIM) for h in some]
    k, v = [k_ref[memory, x] for x in at], [v_ref[memory, x] for x in at]
    scores = [lax.dot_general(q[h], k[h], NT, preferred_element_type=F32) * SCALE for h in some]
    dattention = [lax.dot_general(g[h], v[h], NT, preferred_element_type=F32) for h in some]
    raised = [jnp.exp(x - jnp.max(x, -1, keepdims=True)) for x in scores]
    attention = [x * (1.0 / jnp.sum(x, -1, keepdims=True)) for x in raised]
    mean = [jnp.sum(attention[h] * dattention[h], -1, keepdims=True) for h in some]
    dscores = [(attention[h] * (dattention[h] - mean[h])).astype(BF16) for h in some]
    gq = [jnp.dot(dscores[h], k[h], preferred_element_type=F32) * SCALE for h in some]
    for h in some:
        gk = lax.dot_general(dscores[h], q[h], TN, preferred_element_type=F32) * SCALE
        gk_ref[memory, at[h]] = gk.astype(BF16)
    for h in some:
        gv = lax.dot_general(attention[h].astype(BF16), g[h], TN, preferred_element_type=F32)
        gv_ref[memory, at[h]] = gv.astype(BF16)
    return gq


def neighbour_terms(gk_ref, gv_ref, wk_ref, wv_ref, found, term_s, away_ref, own_ref):
    term = lax.dot_general(gk_ref[...], wk_ref[...], NT, preferred_element_type=F32)
    term = term + lax.dot_general(gv_ref[...], wv_ref[...], NT, preferred_element_type=F32)
    term_s[...] = term.astype(BF16)
    for at, (core, place, rank) in enumerate(found):
        spot = pl.ds(at * R, R)
        for which, ref in ((0, own_ref), (1, away_ref)):

            @pl.when(core == which)
            def _(spot=spot, place=place, rank=rank, ref=ref):
                ref[place, rank] = term_s[spot]


def attend_kernel(*refs):
    shard_ref, fars, k_near, v_near, wk_ref, wv_ref, q_ref, g_ref = refs[0], refs[1:5], *refs[5:11]
    k_ref, v_ref, gq_ref, away_ref, own_ref = refs[11:16]
    mem_s, k_far, v_far, k_s, v_s, gk_s, gv_s, term_s = refs[16:]
    rows, width = q_ref.shape
    spans = rows // CH
    base = rows * width // HDIM
    for slot, far in enumerate(fars):
        for j in range(DE // HDIM):
            part = far[pl.ds(base + j * R, R)]
            mem_s[pl.ds(slot * R, R), pl.ds(j * HDIM, HDIM)] = part
    k_far[...] = jnp.dot(mem_s[...], wk_ref[...], preferred_element_type=F32).astype(BF16)
    v_far[...] = jnp.dot(mem_s[...], wv_ref[...], preferred_element_type=F32).astype(BF16)
    found = places_of(shard_ref)
    for request, (core, place, rank) in enumerate(found):
        spot = pl.ds(request * R, R)

        @pl.when(place == 2)
        def _(spot=spot, slot=core * 2 + rank):
            source = pl.ds(pl.multiple_of(slot * R, R), R)
            k_s[spot], v_s[spot] = k_far[source], v_far[source]

        @pl.when(place != 2)
        def _(spot=spot, slot=(core * 3 + jnp.minimum(place, 2)) * 2 + rank):
            source = pl.ds(pl.multiple_of(slot * R, R), R)
            k_s[spot], v_s[spot] = k_near[source], v_near[source]

    heads = [pl.ds(h * HDIM, HDIM) for h in range(width // HDIM)]
    for c in range(spans - 1):
        span, memory = pl.ds(c * CH, CH), pl.ds(c * K * R, K * R)
        q, g = [q_ref[span, x] for x in heads], [g_ref[span, x] for x in heads]
        gq = span_gradients(q, g, k_s, v_s, memory, gk_s, gv_s)
        for x, value in zip(heads, gq):
            gq_ref[span, x] = value
    memory = pl.ds((spans - 1) * K * R, K * R)
    k_ref[...], v_ref[...] = k_s[memory], v_s[memory]
    first = found[: (spans - 1) * K]
    neighbour_terms(gk_s, gv_s, wk_ref, wv_ref, first, term_s, away_ref, own_ref)


def last_kernel(*refs):
    shard_ref, q_ref, g_ref, tail_ref, k_ref, v_ref, wk_ref, wv_ref, gq_in = refs[:9]
    gq_ref, away_ref, own_ref = refs[11:14]
    gk_s, gv_s, term_s = refs[14:]
    rows, width = q_ref.shape
    last = rows - CH
    heads = [pl.ds(h * HDIM, HDIM) for h in range(width // HDIM)]
    first_row = lax.broadcasted_iota(jnp.int32, (CH, HDIM), 0) == 0
    q, g = (
        [jnp.where(first_row, ref[last:, x], tail_ref[item, :, x]) for x in heads]
        for item, ref in enumerate((q_ref, g_ref))
    )
    gq = span_gradients(q, g, k_ref, v_ref, pl.ds(0, K * R), gk_s, gv_s)
    gq_ref[:last] = gq_in[...].astype(BF16)
    for x, value in zip(heads, gq):
        gq_ref[last:, x] = value.astype(BF16)
    found = places_of(shard_ref)[-K:]
    neighbour_terms(gk_s, gv_s, wk_ref, wv_ref, found, term_s, away_ref, own_ref)


def cross_kernel(gq_ref, w_ref, away_ref, own_ref):
    me = lax.axis_index("db")
    width = gq_ref.shape[1]
    for core, out in ((1, away_ref), (0, own_ref)):
        for place in range(4):
            spot = pl.multiple_of(source_of(me, core, place) * width, width)
            out[place] = lax.dot_general(
                gq_ref[...], w_ref[pl.ds(spot, width), :], NT, preferred_element_type=F32
            ).astype(BF16)


def scatter_kernel(label_ref, parts_ref, out_ref):
    out_ref[...] = jnp.zeros_like(out_ref)
    width = out_ref.shape[2]

    def item(i, carry):
        row = label_ref[i]

        @pl.when(row >= 0)
        def _():
            out_ref[row] += parts_ref[i][:, :width].astype(F32)

        return carry

    lax.fori_loop(0, parts_ref.shape[0], item, 0)


def after(x, token):
    return x + jnp.where(token > 0, -0.0, 0.0).astype(x.dtype)


def add(*parts):
    return functools.reduce(lambda a, b: a + b, [x.astype(F32) for x in parts])


def far_sums(own, got, half):
    return add(own[2][:half], got[2][:half]), add(own[2][half:], got[2][half:])


def near_sums(own, got, half, far_up, far_down):
    nxt = [add(own[1][:half], got[1][:half], far_up), add(own[1][half:], got[1][half:])]
    prv = [add(own[3][:half], got[3][:half]), add(own[3][half:], got[3][half:], far_down)]
    return jnp.concatenate(nxt, 0), jnp.concatenate(prv, 0)


def per_device(
    states, cotangent, w_query, w_key, w_value, w_out, database, neighbour_shard, neighbour_row
):
    rows, width = states.shape
    spans = rows // CH
    limit = pltpu.CompilerParams(vmem_limit_bytes=20 * 2**20)
    shards, named_rows = neighbour_shard.T, neighbour_row.T
    peers = lax.axis_size("ctx")

    given_rows = rows * width // HDIM + R * DE // HDIM
    *given, label = pl.pallas_call(
        load_kernel,
        name="load",
        out_shape=(shape((given_rows, HDIM)),) * 2 + (shape((CAP, 8, 128), F32),),
        in_specs=[SMEM, SMEM, ANY, ANY, ANY],
        out_specs=(VMEM,) * 3,
        scratch_shapes=[pltpu.SemaphoreType.DMA((2 * (width + DE) // HDIM,))],
    )(shards, named_rows, states, cotangent, database)
    *held, done = pl.pallas_call(
        hold_kernel,
        name="hold",
        out_shape=(shape(w_query.shape), shape(w_out.shape), shape(label.shape, F32)),
        in_specs=[VMEM, HBM, HBM],
        out_specs=(VMEM,) * 3,
        scratch_shapes=[pltpu.SemaphoreType.DMA((2,))],
        compiler_params=limit,
    )(label, w_query, w_out)
    prv_a, nxt_b = up(given[0]), down(given[1])
    prv_b, nxt_a = up(given[1]), down(given[0])
    token = done[0, :1]
    far_a, far_b = up(after(prv_a, token)), down(after(nxt_b, token))
    near = (*given, nxt_a, nxt_b, prv_a, prv_b)
    near = near + tuple(across(x) for x in given)
    near = near + (across(after(nxt_a, token)), across(after(nxt_b, prv_b[:1])))
    near = near + (across(after(prv_a, nxt_a[:1])), across(after(prv_b, token)))
    partial, *near_states = pl.pallas_call(
        near_kernel,
        name="near",
        out_shape=(shape((2, rows, width), F32),) + (shape((12 * R, width)),) * 2,
        in_specs=[VMEM] * 16,
        out_specs=(VMEM,) * 3,
        scratch_shapes=[pltpu.VMEM((2, rows, 8 * width), BF16), pltpu.VMEM((12 * R, DE), BF16)],
        compiler_params=limit,
        cost_estimate=cost(1, 1),
    )(*near, *held, w_key, w_value)
    token = partial[0, :1, :HDIM]
    far_a, far_b = after(far_a, token), after(far_b, token)
    fars = (far_a, far_b, across(far_a), across(far_b))
    query, grad_out, tails = pl.pallas_call(
        project_kernel,
        name="project",
        out_shape=(shape((rows, width)), shape((rows, width)), shape((2, CH, width))),
        in_specs=[VMEM] * 7,
        out_specs=(VMEM,) * 3,
        scratch_shapes=[pltpu.VMEM((rows, width), BF16)],
        compiler_params=limit,
        cost_estimate=cost(8 * rows * width * width, 2**23),
    )(*fars, *held, partial)
    tails = along_ctx(tails, -1)
    positions, slots_of = spans * K * R, shape((4, CAP, R, DE))
    most = positions - K * R
    *last, away, own = pl.pallas_call(
        attend_kernel,
        name="attend",
        out_shape=(shape((K * R, width)), shape((K * R, width)), shape((rows - CH, width), F32))
        + (slots_of, slots_of),
        in_specs=[SMEM] + [VMEM] * 10,
        out_specs=(VMEM,) * 5,
        scratch_shapes=[
            pltpu.VMEM((4 * R, DE), BF16),
            pltpu.VMEM((4 * R, width), BF16),
            pltpu.VMEM((4 * R, width), BF16),
            pltpu.VMEM((positions, width), BF16),
            pltpu.VMEM((positions, width), BF16),
            pltpu.VMEM((most, width), BF16),
            pltpu.VMEM((most, width), BF16),
            pltpu.VMEM((most, DE), BF16),
        ],
        compiler_params=limit,
        cost_estimate=cost(8 * positions * DE * width, 2**23),
    )(shards, *fars, *near_states, w_key, w_value, query, grad_out)
    grad_query, away, own = pl.pallas_call(
        last_kernel,
        name="last",
        out_shape=(shape((rows, width)), slots_of, slots_of),
        in_specs=[SMEM] + [VMEM] * 8 + [VMEM] * 2,
        out_specs=(VMEM,) * 3,
        scratch_shapes=[
            pltpu.VMEM((K * R, width), BF16),
            pltpu.VMEM((K * R, width), BF16),
            pltpu.VMEM((K * R, DE), BF16),
        ],
        input_output_aliases={9: 1, 10: 2},
        compiler_params=limit,
        cost_estimate=cost(2 * positions * DE * width, 2**22),
    )(shards, query, grad_out, tails, last[0], last[1], w_key, w_value, last[2], away, own)
    got, half = across(away), CAP // 2
    far_up, far_down = far_sums(own, got, half)
    far_up, far_down = up(far_up.astype(BF16)), down(far_down.astype(BF16))
    nxt, prv = (x.astype(BF16) for x in near_sums(own, got, half, far_up, far_down))
    slots = add(own[0], got[0], up(nxt), down(prv)).astype(BF16)
    block = R // peers
    spread = slots.reshape(CAP, peers, block, DE).transpose(1, 0, 2, 3)
    labels = jnp.broadcast_to(label.astype(BF16), (peers,) + label.shape)
    spread = jnp.concatenate([spread, labels], -1)
    parts = lax.all_to_all(spread, "ctx", 0, 0, tiled=True)
    parts = parts.reshape(peers * CAP, block, DE + label.shape[-1])
    labels = parts[:, 0, DE].astype(jnp.int32)
    cross_away, cross_own = pl.pallas_call(
        cross_kernel,
        name="cross",
        out_shape=(shape((4, rows, width)), shape((4, rows, width))),
        in_specs=[VMEM] * 2,
        out_specs=(VMEM, VMEM),
        compiler_params=limit,
        cost_estimate=cost(2 * rows * width * 8 * width, 2**23),
    )(grad_query, held[0])
    cross_got, half = across(cross_away), rows // 2
    far_up, far_down = far_sums(cross_own, cross_got, half)
    far_up, far_down = up(far_up.astype(BF16)), down(far_down.astype(BF16))
    nxt, prv = near_sums(cross_own, cross_got, half, far_up, far_down)
    nxt, prv = nxt.astype(BF16), prv.astype(BF16)
    cross = add(cross_own[0], cross_got[0], up(nxt), down(prv))
    keep = rows - BORDER
    carried = along_ctx(cross[keep:].astype(BF16), 1).astype(F32)
    grad_states = cotangent.astype(F32) + jnp.concatenate([carried, cross[:keep]], 0)
    grad_database = pl.pallas_call(
        scatter_kernel,
        name="scatter",
        out_shape=shape((database.shape[0], block, DE), F32),
        in_specs=[SMEM, VMEM],
        out_specs=VMEM,
        compiler_params=limit,
        cost_estimate=cost(2**38, 2**32),
    )(labels, parts)
    return grad_states, grad_database


def solution(mesh):
    in_specs = (
        P("ctx", "db"),
        P("ctx", "db"),
        P(None, "db"),
        P(None, "db"),
        P(None, "db"),
        P("db", None),
        P("db", None, None),
        P("ctx", None),
        P("ctx", None),
    )
    out_specs = (P("ctx", "db"), P("db", "ctx", None))
    return jax.shard_map(
        per_device, mesh=mesh, in_specs=in_specs, out_specs=out_specs, check_vma=False
    )
```
